512 devices in a mesh: freq: 128 (over z, x, core), rcv: 4 (over y).
Axes of the slice: x: 4, y: 4, z: 16, core: 2. Of those that a mesh axis runs over, the one named last changes fastest.
Arguments:
- recorded: float32 [1024, 64, 1024], P(('rcv', 'freq')), may hold values from -32 to 32
- kernel: bfloat16 [256, 1024, 2, 1024], P('freq', None, None, 'rcv'), may hold values from -0.125 to 0.125
- freq_index: int32 [256], replicated, may hold values from 1 to 511, as said below
Outputs:
- solution: float32 [1024, 64, 1024], P(('rcv', 'freq'))
- normal_residual: float32 [1024, 64, 1024], P(('rcv', 'freq'))
The draws below stay inside these ranges and needn't reach their ends.
Inputs may be any that keep to these rules, and one draw needn't show every extreme that they name: `freq_index`: 256 distinct values; both 1 and 511 appear.
All inputs are finite; a program needn't handle non-finite values.
Results may differ from the reference program's by a relative error of at most 0.017.
Values may be sent and summed in bfloat16 or wider, within the bound.
No kernel may reach another device: no remote copies, remote signals or barrier semaphores. Data moves between devices by JAX's collectives and lax.ppermute only.
A program may use at most 64 MiB of HBM per device.

```python
import math
import jax
import jax.numpy as jnp
from jax import lax

NT = 1024
V = 64
ITERS = 2
S = 1024
R = 1024
NF = 256


def draw_recorded(key, part):
    key = jax.random.fold_in(key, 11)
    first, second = jax.random.split(key, 2)
    rising = 1.0 + 2.0 * jnp.arange(S, dtype=jnp.float32) / (S - 1)
    spread = jnp.exp(jax.random.uniform(second, (S, V, 1), jnp.float32) * math.log(10.0))
    scale = spread * rising[:, None, None]
    base = jnp.clip(jax.random.normal(first, (S, V, NT), jnp.float32), -4.0, 4.0)
    return (0.25 * base * scale).astype(jnp.float32)


def draw_freq_index(key, part):
    key = jax.random.fold_in(key, 23)
    first, second = jax.random.split(key)
    inner = jax.random.permutation(first, NT // 2 - 3)[:NF - 2] + 2
    ends = jnp.array([1, NT // 2 - 1], dtype=jnp.int32)
    full = jnp.concatenate([ends, inner.astype(jnp.int32)])
    order = jax.random.permutation(second, NF)
    return full[order].astype(jnp.int32)


def block_levels(key, shape, cuts, smallest, largest):
    level = 1.0
    for position, parts in cuts:
        heights = jax.random.uniform(jax.random.fold_in(jax.random.fold_in(key, 6), position), (parts,), jnp.float32, smallest / len(cuts), largest / len(cuts))
        level = level * jnp.repeat(jnp.exp(heights), shape[position] // parts).reshape((-1,) + (1,) * (len(shape) - 1 - position))
    return level


def scatter_about(key, shape, scale, reach, pieces=(), held_as=jnp.bfloat16):
    values = jax.random.normal(key, shape, jnp.float32) * scale
    if len(pieces) > 0:
        values = block_levels(key, shape, pieces, -0.22, 0.18) * values
    return jnp.clip(values, min=-reach, max=reach).astype(held_as)


def setup_inputs(seed: int = 0) -> dict:
    keys = jax.random.split(jax.random.key(seed), 4)
    recorded = draw_recorded(jax.random.fold_in(keys[3], 71), 0)
    kernel = scatter_about(keys[1], (NF, S, 2, R), (2 * R) ** -0.5, 0.125, ((0, 128), (3, 4)))
    freq_index = draw_freq_index(jax.random.fold_in(keys[3], 71), 0)
    return {"recorded": recorded, "kernel": kernel, "freq_index": freq_index}


HIGH = lax.Precision.HIGHEST

def dft_table(freq_index, samples):
    times = jnp.arange(samples, dtype=jnp.int32)
    phase = freq_index.astype(jnp.int32)[:, None] * times[None, :] % samples
    angle = 2.0 * jnp.pi / samples * phase.astype(jnp.float32)
    factor = 1.0 / jnp.sqrt(jnp.float32(samples))
    return jnp.stack([jnp.cos(angle) * factor, -jnp.sin(angle) * factor])

def to_spectrum(table, field):
    spectrum = jnp.einsum('pkt,rvt->krpv', table, field, precision=HIGH)
    return spectrum.reshape(spectrum.shape[0], spectrum.shape[1], -1)

def to_traces(table, spectrum):
    rows, kept, width = spectrum.shape
    split = spectrum.reshape(rows, kept, 2, width // 2)
    return jnp.einsum('rkpv,pkt->rvt', split, table, precision=HIGH)

def forward_op(kernel, table, field):
    rounded = to_spectrum(table, field).astype(jnp.bfloat16)

    def per_freq(pair):
        kern, block = pair
        flat = kern.reshape(kern.shape[0], -1)
        half = block.shape[1] // 2
        turned = jnp.concatenate([-block[:, half:], block[:, :half]], axis=1)
        stacked = jnp.concatenate([block, turned], axis=0)
        return jnp.dot(flat, stacked, preferred_element_type=jnp.float32)
    images = lax.map(per_freq, (kernel, rounded))
    return to_traces(table, jnp.transpose(images, (1, 0, 2)))

def adjoint_op(kernel, table, field):
    rounded = to_spectrum(table, field).astype(jnp.bfloat16)

    def per_freq(pair):
        kern, block = pair
        flat = kern.reshape(kern.shape[0], -1)
        count = flat.shape[1] // 2
        half = block.shape[1] // 2
        product = jnp.dot(flat.T, block, preferred_element_type=jnp.float32)
        real_part = product[:count, :half] + product[count:, half:]
        imag_part = product[:count, half:] - product[count:, :half]
        return jnp.concatenate([real_part, imag_part], axis=1)
    images = lax.map(per_freq, (kernel, rounded))
    return to_traces(table, jnp.transpose(images, (1, 0, 2)))

def vector_norm(field):
    return jnp.sqrt(jnp.sum(field * field))

def rotate(solution, direction, right_vec, diag_est, residual_est, beta_norm, alpha_norm):
    rotation_norm = jnp.sqrt(diag_est * diag_est + beta_norm * beta_norm)
    cos_term = diag_est / rotation_norm
    sin_term = beta_norm / rotation_norm
    coupling = sin_term * alpha_norm
    diag_next = -cos_term * alpha_norm
    step_weight = cos_term * residual_est
    residual_next = sin_term * residual_est
    solution = solution + step_weight / rotation_norm * direction
    direction = right_vec - coupling / rotation_norm * direction
    return (solution, direction, diag_next, residual_next)

def reference(recorded, kernel, freq_index):
    table = dft_table(freq_index, recorded.shape[2])
    beta_norm = vector_norm(recorded)
    left_vec = recorded / beta_norm
    right_vec = adjoint_op(kernel, table, left_vec)
    alpha_norm = vector_norm(right_vec)
    right_vec = right_vec / alpha_norm
    direction = right_vec
    solution = jnp.zeros_like(right_vec)
    residual_est = beta_norm
    diag_est = alpha_norm
    for step in range(ITERS):
        left_vec = forward_op(kernel, table, right_vec) - alpha_norm * left_vec
        beta_norm = vector_norm(left_vec)
        left_vec = left_vec / beta_norm
        right_vec = adjoint_op(kernel, table, left_vec) - beta_norm * right_vec
        alpha_norm = vector_norm(right_vec)
        right_vec = right_vec / alpha_norm
        solution, direction, diag_est, residual_est = rotate(solution, direction, right_vec, diag_est, residual_est, beta_norm, alpha_norm)
    return (solution, residual_est * diag_est * right_vec)
```

```python
import functools
import math

import jax
import jax.numpy as jnp
from jax import lax
from jax.experimental import pallas as pl
from jax.experimental.pallas import tpu as pltpu
from jax.sharding import PartitionSpec as P

Y = 4
HV = 32
HIGH = lax.Precision.HIGHEST
MIB = 1024 * 1024


def dft_kernel(fr_ref, rec_ref, tab_ref, out_ref, norm_ref):
    kept = fr_ref.shape[0]
    samples = rec_ref.shape[1]
    chunks = samples // 128
    unit = 2.0 * math.pi / samples
    fr = fr_ref[...]
    lane = lax.broadcasted_iota(jnp.int32, (kept, 128), 1)
    fine = (fr * lane & (samples - 1)).astype(jnp.float32) * unit
    coarse = (fr * (lane * 128) & (samples - 1)).astype(jnp.float32) * unit
    cos_f, sin_f = jnp.cos(fine), jnp.sin(fine)
    factor = 1.0 / math.sqrt(samples)
    cos_c, sin_c = jnp.cos(coarse) * factor, jnp.sin(coarse) * factor
    for a in range(chunks):
        ca, sa = cos_c[:, a : a + 1], sin_c[:, a : a + 1]
        tab_ref[0, :, a * 128 : (a + 1) * 128] = ca * cos_f - sa * sin_f
        tab_ref[1, :, a * 128 : (a + 1) * 128] = -(sa * cos_f + ca * sin_f)
    rec = rec_ref[...]
    norm_ref[...] = jnp.sum(rec * rec, axis=(0, 1), keepdims=True)
    spec = [
        lax.dot_general(
            tab_ref[p], rec, (((1,), (1,)), ((), ())), precision=HIGH, preferred_element_type=jnp.float32
        )
        for p in range(2)
    ]
    for c in range(2):
        parts = [spec[p][:, (2 * src + c) * HV : (2 * src + c + 1) * HV] for src in range(2) for p in range(2)]
        out_ref[c] = jnp.concatenate(parts, axis=1).astype(jnp.bfloat16)


def quarter_turn(x):
    width = x.shape[1]
    even = lax.broadcasted_iota(jnp.int32, x.shape, 1) % 2 == 0
    return jnp.where(even, pltpu.roll(x, width - 1, 1), -pltpu.roll(x, 1, 1))


def length_of(x):
    return jnp.sqrt(jnp.sum(x * x, axis=(0, 1), keepdims=True))


def inverse_of(x):
    return jnp.where(x > 1e-30, 1.0 / jnp.maximum(x, 1e-30), 0.0)


def krylov_kernel(idx_ref, norm_ref, *refs):
    u_refs, k_refs, g_refs = refs[:4], refs[4:12], refs[12:16]
    kmat, u_rows, u_all, q_rows, g_rows, sems = refs[16:]
    devices = u_refs[0].shape[0]
    half = devices // 2
    y, core = idx_ref[0], idx_ref[1]

    copies = []
    for j in range(8):
        side = core if j < 4 else 1 - core
        start = pl.multiple_of(side * (4 * devices) + (j % 4) * devices, devices)
        copies.append(pltpu.make_async_copy(k_refs[j], kmat.at[:, pl.ds(start, devices)], sems.at[j]))
    for copy in copies:
        copy.start()

    for o in range(4):
        block = u_refs[o][...].astype(jnp.float32)
        for g in range(4):
            u_rows[pl.ds(g, devices, stride=4), 0:HV] = block[:, g * HV : (g + 1) * HV]
        turned = u_rows[...].T[0:HV]
        start = pl.multiple_of(lax.rem(y + 4 - o, 4) * (4 * devices), 4 * devices)
        u_all[:, pl.ds(start, 4 * devices)] = turned

    for copy in copies:
        copy.wait()

    def adjoint(p):
        both = jnp.concatenate([p, quarter_turn(p)], axis=0).astype(jnp.bfloat16)
        return 0.5 * jnp.dot(both, kmat[...], preferred_element_type=jnp.float32)

    def forward(q):
        w = lax.dot_general(
            q.astype(jnp.bfloat16), kmat[...], (((1,), (1,)), ((), ())), preferred_element_type=jnp.float32
        )
        return 0.5 * (w[:HV] - quarter_turn(w[HV:]))

    u = u_all[...]
    length = length_of(u)
    scale = inverse_of(length)
    g1 = adjoint(u) * scale
    a1 = length_of(g1)
    q1 = g1 * inverse_of(a1)
    h2 = forward(q1) - (a1 * scale) * u
    b2 = length_of(h2)
    p2 = h2 * inverse_of(b2)
    g2 = adjoint(p2) - b2 * q1
    a2 = length_of(g2)
    q2 = g2 * inverse_of(a2)
    h3 = forward(q2) - a2 * p2
    b3 = length_of(h3)
    p3 = h3 * inverse_of(b3)
    g3 = adjoint(p3) - b3 * q2
    a3 = length_of(g3)
    q3 = g3 * inverse_of(a3)

    lane = lax.broadcasted_iota(jnp.int32, (1, 128), 1)
    slot = lane % 8
    values = jnp.zeros((1, 128), jnp.float32)
    for n, value in enumerate((math.sqrt(2.0) * length, a1, b2, a2, b3, a3, norm_ref[...])):
        values = jnp.where(slot == n, value, values)
    hi = values.astype(jnp.bfloat16).astype(jnp.float32)
    rest = values - hi
    mid = rest.astype(jnp.bfloat16).astype(jnp.float32)
    low = rest - mid
    scalars = jnp.where(lane < 8, hi, jnp.where(lane < 16, mid, jnp.where(lane < 24, low, 0.0)))

    for o in range(4):
        g_rows[o, pl.ds(3, devices, stride=4), :] = jnp.broadcast_to(scalars, (devices, 128))
    for pair in range(2):
        first, second = ((q1, q2), (q3, q3))[pair]
        q_rows[...] = jnp.concatenate([first, second], axis=0).T
        even = q_rows[pl.ds(0, 4 * devices, stride=2), :]
        odd = q_rows[pl.ds(1, 4 * devices, stride=2), :]
        for inner in range(2 - pair):
            lanes = slice(inner * 64, (inner + 1) * 64)
            both = jnp.concatenate([even[:, lanes], odd[:, lanes]], axis=1)
            vec = 2 * pair + inner
            for side in range(2):
                for o in range(4):
                    j = side * 4 + o
                    g_rows[o, pl.ds(side * half * 4 + vec, half, stride=4), :] = both[j * half : (j + 1) * half]
    for o in range(4):
        g_refs[o][...] = g_rows[o].astype(jnp.bfloat16)


def total(x):
    return jnp.sum(x)


def reduced_lsqr(scal):
    s, a1, b2, a2, b3, a3, rec = [scal[..., n] for n in range(7)]
    beta = jnp.sqrt(total(rec))
    y11 = s / beta
    w1 = jnp.sqrt(jnp.maximum(1.0 - total(y11 * y11), 0.0))
    x = a1 * y11
    alpha = jnp.sqrt(total(x * x))
    x11 = x / alpha
    res, diag = beta, alpha
    y21, y22, w2 = a1 * x11 - alpha * y11, b2 * x11, -alpha * w1
    beta = jnp.sqrt(total(y21 * y21 + y22 * y22) + w2 * w2)
    y21, y22, w2 = y21 / beta, y22 / beta, w2 / beta
    x21, x22 = a1 * y21 + b2 * y22 - beta * x11, a2 * y22
    alpha = jnp.sqrt(total(x21 * x21 + x22 * x22))
    x21, x22 = x21 / alpha, x22 / alpha

    def rotate(res, diag, beta, alpha):
        rho = jnp.sqrt(diag * diag + beta * beta)
        c, sn = diag / rho, beta / rho
        return c * res / rho, sn * alpha / rho, sn * res, -c * alpha

    step, couple, res, diag = rotate(res, diag, beta, alpha)
    sol1 = step * x11
    dir1, dir2 = x21 - couple * x11, x22
    y31, y32, y33 = a1 * x21 - alpha * y21, b2 * x21 + a2 * x22 - alpha * y22, b3 * x22
    w3 = -alpha * w2
    beta = jnp.sqrt(total(y31 * y31 + y32 * y32 + y33 * y33) + w3 * w3)
    y31, y32, y33 = y31 / beta, y32 / beta, y33 / beta
    x31 = a1 * y31 + b2 * y32 - beta * x21
    x32 = a2 * y32 + b3 * y33 - beta * x22
    x33 = a3 * y33
    alpha = jnp.sqrt(total(x31 * x31 + x32 * x32 + x33 * x33))
    step, couple, res, diag = rotate(res, diag, beta, alpha)
    last = res * diag / alpha
    return (sol1 + step * dir1, step * dir2), (last * x31, last * x32, last * x33)


def body(devices, recorded, kernel, freq_index):
    share, virtual, samples = recorded.shape
    f = lax.axis_index("freq")
    y = lax.axis_index("rcv")
    core = f % 2
    columns = devices // 2
    kept = freq_index.shape[0]
    sources = kernel.shape[1]
    swap = [(i, i ^ 1) for i in range(devices)]

    def shift(o):
        return [(i, (i + o) % Y) for i in range(Y)]

    low, high = kernel[..., :devices], kernel[..., devices:]
    own = jnp.where(core == 0, low, high).reshape(2, 2 * sources, devices)
    send = jnp.where(core == 0, high, low).reshape(2, 2 * sources, devices)
    other = lax.ppermute(send, "freq", swap)

    def block(phi):
        mine = lax.dynamic_index_in_dim(own, phi % 2, 0, keepdims=False)
        theirs = lax.dynamic_index_in_dim(other, phi % 2, 0, keepdims=False)
        return jnp.where(phi // 2 == core, mine, theirs)

    blocks = [block(y)] + [lax.ppermute(block((y + o) % Y), "rcv", shift(o)) for o in range(1, Y)]
    blocks = blocks + [lax.ppermute(b, "freq", swap) for b in blocks]

    fr = freq_index.reshape(columns, Y)
    fr = lax.dynamic_slice_in_dim(jnp.concatenate([fr, fr], axis=1), y, Y, axis=1)
    table, spec, rec_norm = pl.pallas_call(
        dft_kernel,
        out_shape=(
            jax.ShapeDtypeStruct((2, kept, samples), jnp.float32),
            jax.ShapeDtypeStruct((2, kept, 128), jnp.bfloat16),
            jax.ShapeDtypeStruct((1, 1), jnp.float32),
        ),
        compiler_params=pltpu.CompilerParams(vmem_limit_bytes=32 * MIB),
        name="dft",
    )(fr.reshape(kept, 1), recorded.reshape(share * virtual, samples))
    spec = spec.reshape(2, columns, Y, 128).transpose(1, 0, 2, 3).reshape(devices, Y, 128)
    spec = lax.all_to_all(spec, "freq", split_axis=0, concat_axis=0, tiled=True)
    parts = [spec[:, 0]] + [lax.ppermute(spec[:, o], "rcv", shift(o)) for o in range(1, Y)]

    position = jnp.stack([y, core]).astype(jnp.int32)
    vectors = pl.pallas_call(
        krylov_kernel,
        out_shape=tuple(jax.ShapeDtypeStruct((4 * devices, 128), jnp.bfloat16) for _ in range(Y)),
        in_specs=[pl.BlockSpec(memory_space=pltpu.SMEM), pl.BlockSpec(memory_space=pltpu.VMEM)]
        + [pl.BlockSpec(memory_space=pltpu.VMEM)] * 4
        + [pl.BlockSpec(memory_space=pl.ANY)] * 8,
        out_specs=tuple(pl.BlockSpec(memory_space=pltpu.VMEM) for _ in range(Y)),
        scratch_shapes=[
            pltpu.VMEM((2 * sources, 8 * devices), jnp.bfloat16),
            pltpu.VMEM((4 * devices, 128), jnp.float32),
            pltpu.VMEM((HV, 2 * sources), jnp.float32),
            pltpu.VMEM((8 * devices, 128), jnp.float32),
            pltpu.VMEM((Y, 4 * devices, 128), jnp.float32),
            pltpu.SemaphoreType.DMA((8,)),
        ],
        compiler_params=pltpu.CompilerParams(vmem_limit_bytes=32 * MIB),
        name="krylov",
    )(position, rec_norm, *parts, *blocks)
    back = [vectors[0]] + [lax.ppermute(vectors[o], "rcv", shift(Y - o)) for o in range(1, Y)]
    back = jnp.stack([b.reshape(devices, 4, 128) for b in back], axis=1)
    back = lax.all_to_all(back, "freq", split_axis=0, concat_axis=0, tiled=True)

    scal = back[:, :, 3, :24].astype(jnp.float32)
    scal = scal[..., :8] + scal[..., 8:16] + scal[..., 16:24]
    sol_c, res_c = reduced_lsqr(scal)
    vecs = [back[:, :, n].astype(jnp.float32) for n in range(3)]
    root = math.sqrt(2.0)
    sol = sum((root * w)[..., None] * v for w, v in zip(sol_c, vecs))
    res = sum((root * w)[..., None] * v for w, v in zip(res_c, vecs))
    table = table.reshape(2, columns, Y, samples)

    def to_time(x):
        x = x.reshape(columns, 2, Y, share, 2, HV)
        return jnp.einsum("zcorqv,qzot->rcvt", x, table, precision=HIGH).reshape(share, virtual, samples)

    return to_time(sol), to_time(res)


def solution(mesh):
    in_specs = (P(("rcv", "freq"), None, None), P("freq", None, None, "rcv"), P())
    out_specs = (P(("rcv", "freq"), None, None), P(("rcv", "freq"), None, None))
    run = functools.partial(body, mesh.shape["freq"])
    return jax.shard_map(run, mesh=mesh, in_specs=in_specs, out_specs=out_specs, check_vma=False)
```

```python
import functools
import math

import jax
import jax.numpy as jnp
from jax import lax
from jax.experimental import pallas as pl
from jax.experimental.pallas import tpu as pltpu
from jax.sharding import Mesh, PartitionSpec as P

Y = 4
GROUP = 8
HV = 32
EXTRA = 16
HIGH = lax.Precision.HIGHEST
MIB = 1024 * 1024
COLUMN = ("core", "rcv")


def dft_kernel(fr_ref, rec_ref, thi_ref, tlo_ref, out_ref, norm_ref, table, rows):
    columns = fr_ref.shape[0]
    kept = Y * columns
    samples = rec_ref.shape[1]
    unit = 2.0 * math.pi / samples
    fr = jnp.concatenate([fr_ref[:, phi : phi + 1] for phi in range(Y)], axis=0)
    lane = lax.broadcasted_iota(jnp.int32, (kept, 128), 1)
    fine = (fr * lane & (samples - 1)).astype(jnp.float32) * unit
    coarse = (fr * (lane * 128) & (samples - 1)).astype(jnp.float32) * unit
    cos_f, sin_f = jnp.cos(fine), jnp.sin(fine)
    factor = 1.0 / math.sqrt(samples)
    cos_c, sin_c = jnp.cos(coarse) * factor, jnp.sin(coarse) * factor
    for a in range(samples // 128):
        ca, sa = cos_c[:, a : a + 1], sin_c[:, a : a + 1]
        part = slice(a * 128, (a + 1) * 128)
        for p, value in enumerate((ca * cos_f - sa * sin_f, -(sa * cos_f + ca * sin_f))):
            table[p, :, part] = value
            top = value.astype(jnp.bfloat16)
            thi_ref[p, :, part] = top
            tlo_ref[p, :, part] = (value - top.astype(jnp.float32)).astype(jnp.bfloat16)
    rec = rec_ref[...]
    norm_ref[...] = jnp.sum(rec * rec, axis=(0, 1), keepdims=True)
    spec = [
        lax.dot_general(table[p], rec, (((1,), (1,)), ((), ())), precision=HIGH, preferred_element_type=jnp.float32)
        for p in range(2)
    ]
    for c in range(2):
        parts = [spec[p][:, (2 * src + c) * HV : (2 * src + c + 1) * HV] for src in range(2) for p in range(2)]
        both = jnp.concatenate(parts, axis=1)
        for phi in range(Y):
            rows[pl.ds(c * Y + phi, columns, stride=GROUP), :] = both[phi * columns : (phi + 1) * columns]
    out_ref[...] = rows[...].astype(jnp.bfloat16)


def quarter_turn(x):
    width = x.shape[1]
    even = lax.broadcasted_iota(jnp.int32, x.shape, 1) % 2 == 0
    return jnp.where(even, pltpu.roll(x, width - 1, 1), -pltpu.roll(x, 1, 1))


def total(x):
    return jnp.sum(x, axis=(0, 1), keepdims=True)


def length_of(x):
    return jnp.sqrt(total(x * x))


def inverse_of(x):
    return jnp.where(x > 1e-30, 1.0 / jnp.maximum(x, 1e-30), 0.0)


def krylov_kernel(idx_ref, norm_ref, u_ref, *refs):
    k_refs, g_ref = refs[:8], refs[8]
    kmat, u_rows, q_rows, sems = refs[9:]
    columns = u_ref.shape[1]
    width = 2 * columns
    half = columns // 2
    y, core = idx_ref[0], idx_ref[1]

    copies = []
    for j in range(8):
        side = core if j < 4 else 1 - core
        quarter = lax.rem(y + 8 - j % 4 - 2 * side, Y)
        start = pl.multiple_of((side * Y + quarter) * width, width)
        copies.append(pltpu.make_async_copy(k_refs[j], kmat.at[:, pl.ds(start, width)], sems.at[j]))
    for copy in copies:
        copy.start()

    for c in range(2):
        fields = [u_ref[c * Y + ys].astype(jnp.float32) for ys in range(Y)]
        for g in range(4):
            both = jnp.concatenate([block[:, g * HV : (g + 1) * HV] for block in fields], axis=1)
            u_rows[pl.ds(c * 4 + g, columns, stride=8), :] = both
    turned = u_rows[...].T
    u = jnp.concatenate([turned[ys * HV : (ys + 1) * HV] for ys in range(Y)], axis=1)

    for copy in copies:
        copy.wait()

    def adjoint(p):
        both = jnp.concatenate([p, quarter_turn(p)], axis=0).astype(jnp.bfloat16)
        return 0.5 * jnp.dot(both, kmat[...], preferred_element_type=jnp.float32)

    def forward(q):
        w = lax.dot_general(
            q.astype(jnp.bfloat16), kmat[...], (((1,), (1,)), ((), ())), preferred_element_type=jnp.float32
        )
        return 0.5 * (w[:HV] - quarter_turn(w[HV:]))

    length = length_of(u)
    scale = inverse_of(length)
    g1 = adjoint(u) * scale
    a1 = length_of(g1)
    q1 = g1 * inverse_of(a1)
    h2 = forward(q1) - (a1 * scale) * u
    b2 = length_of(h2)
    p2 = h2 * inverse_of(b2)
    g2 = adjoint(p2) - b2 * q1
    a2 = length_of(g2)
    q2 = g2 * inverse_of(a2)
    h3 = forward(q2) - a2 * p2
    b3 = length_of(h3)
    p3 = h3 * inverse_of(b3)
    g3 = adjoint(p3) - b3 * q2
    a3 = length_of(g3)
    q3 = g3 * inverse_of(a3)

    lane = lax.broadcasted_iota(jnp.int32, (EXTRA, 128), 1)
    slot = lax.rem(lane, 64) // GROUP
    values = jnp.zeros((EXTRA, 128), jnp.float32)
    for n, value in enumerate((math.sqrt(2.0) * length, a1, b2, a2, b3, a3, norm_ref[...])):
        values = jnp.where(slot == n, value, values)
    hi = values.astype(jnp.bfloat16).astype(jnp.float32)
    scalars = jnp.where(lane < 64, hi, values - hi)
    scalars = jnp.where(lax.rem(lane, GROUP) == core * Y + y, scalars, 0.0).astype(jnp.bfloat16)

    for pair in range(2):
        first, second = ((q1, q2), (q3, q3))[pair]
        q_rows[...] = jnp.concatenate([first, second], axis=0).T
        for c in range(2):
            for quarter in range(Y):
                for side in range(2):
                    base = (side * Y + quarter) * width + 2 * c
                    even = q_rows[pl.ds(base, half, stride=4), :]
                    odd = q_rows[pl.ds(base + 1, half, stride=4), :]
                    for inner in range(2 - pair):
                        lanes = slice(inner * 64, (inner + 1) * 64)
                        both = jnp.concatenate([even[:, lanes], odd[:, lanes]], axis=1)
                        row = (2 * pair + inner) * columns + side * half
                        g_ref[c * Y + quarter, row : row + half, :] = both.astype(jnp.bfloat16)
    for e in range(GROUP):
        g_ref[e, 3 * columns : 3 * columns + EXTRA, :] = scalars


def reduced_lsqr(s, a1, b2, a2, b3, a3, rec):
    def norm(*parts):
        return jnp.sqrt(total(sum(part * part for part in parts)))

    beta = jnp.sqrt(total(rec))
    y11 = s / beta
    w1 = jnp.sqrt(jnp.maximum(1.0 - total(y11 * y11), 0.0))
    x = a1 * y11
    alpha = norm(x)
    x11 = x / alpha
    res, diag = beta, alpha
    y21, y22, w2 = a1 * x11 - alpha * y11, b2 * x11, -alpha * w1
    beta = jnp.sqrt(total(y21 * y21 + y22 * y22) + w2 * w2)
    y21, y22, w2 = y21 / beta, y22 / beta, w2 / beta
    x21, x22 = a1 * y21 + b2 * y22 - beta * x11, a2 * y22
    alpha = norm(x21, x22)
    x21, x22 = x21 / alpha, x22 / alpha

    def rotate(res, diag, beta, alpha):
        rho = jnp.sqrt(diag * diag + beta * beta)
        c, sn = diag / rho, beta / rho
        return c * res / rho, sn * alpha / rho, sn * res, -c * alpha

    step, couple, res, diag = rotate(res, diag, beta, alpha)
    sol1 = step * x11
    dir1, dir2 = x21 - couple * x11, x22
    y31, y32, y33 = a1 * x21 - alpha * y21, b2 * x21 + a2 * x22 - alpha * y22, b3 * x22
    w3 = -alpha * w2
    beta = jnp.sqrt(total(y31 * y31 + y32 * y32 + y33 * y33) + w3 * w3)
    y31, y32, y33 = y31 / beta, y32 / beta, y33 / beta
    x31 = a1 * y31 + b2 * y32 - beta * x21
    x32 = a2 * y32 + b3 * y33 - beta * x22
    x33 = a3 * y33
    alpha = norm(x31, x32, x33)
    step, couple, res, diag = rotate(res, diag, beta, alpha)
    last = res * diag / alpha
    return (sol1 + step * dir1, step * dir2), (last * x31, last * x32, last * x33)


def traces_kernel(m_ref, thi_ref, tlo_ref, sol_ref, res_ref):
    kept = thi_ref.shape[1]
    samples = thi_ref.shape[2]
    scal = m_ref[3 * GROUP].astype(jnp.float32)
    parts = [
        scal[:, n * GROUP : (n + 1) * GROUP] + scal[:, 64 + n * GROUP : 64 + (n + 1) * GROUP] for n in range(7)
    ]
    sol_c, res_c = reduced_lsqr(*parts)
    root = math.sqrt(2.0)
    sol_c, res_c = [root * w for w in sol_c], [root * w for w in res_c]
    lines = []
    for weights in (sol_c, res_c):
        for c in range(2):
            blocks = []
            for phi in range(Y):
                e = c * Y + phi
                blocks.append(
                    sum(w[:, e : e + 1] * m_ref[3 * e + n].astype(jnp.float32) for n, w in enumerate(weights))
                )
            turned = jnp.concatenate(blocks, axis=0).T
            for rr in range(2):
                lines.append(
                    jnp.concatenate([turned[(2 * rr + q) * HV : (2 * rr + q + 1) * HV] for q in range(2)], axis=1)
                )
    x = jnp.concatenate(lines, axis=0)
    hi = x.astype(jnp.bfloat16)
    lo = (x - hi.astype(jnp.float32)).astype(jnp.bfloat16)
    thi = thi_ref[...].reshape(2 * kept, samples)
    tlo = tlo_ref[...].reshape(2 * kept, samples)

    def dot(a, b):
        return jnp.dot(a, b, preferred_element_type=jnp.float32)

    out = dot(hi, thi) + (dot(hi, tlo) + dot(lo, thi))
    for n, ref in enumerate((sol_ref, res_ref)):
        for c in range(2):
            for rr in range(2):
                row = ((n * 2 + c) * 2 + rr) * HV
                ref[rr, c * HV : (c + 1) * HV, :] = out[row : row + HV]


def body(recorded, kernel, freq_index):
    share, virtual, samples = recorded.shape
    columns = freq_index.shape[0] // Y
    kept = freq_index.shape[0]
    sources = kernel.shape[1]
    width = kernel.shape[3] // 2
    core = lax.axis_index("core")
    y = lax.axis_index("rcv")

    def route(o):
        pairs = []
        for c in range(2):
            for here in range(Y):
                if (here + o) % Y // 2 == c:
                    pairs.append((c * Y + here, (here + o) % Y))
                else:
                    pairs.append((c * Y + here, Y + (here + o + 2) % Y))
        return pairs

    def payload(o):
        mine = lax.dynamic_index_in_dim(kernel, (y + o) % 2, 0, keepdims=False)
        low = (y + o) % Y // 2 == core
        return jnp.where(low, mine[..., :width], mine[..., width:]).reshape(2 * sources, width)

    blocks = [lax.ppermute(payload(o), COLUMN, route(o)) for o in range(Y)]
    blocks = blocks + [lax.ppermute(b, "core", [(0, 1), (1, 0)]) for b in blocks]

    table_hi, table_lo, spec, rec_norm = pl.pallas_call(
        dft_kernel,
        out_shape=(
            jax.ShapeDtypeStruct((2, kept, samples), jnp.bfloat16),
            jax.ShapeDtypeStruct((2, kept, samples), jnp.bfloat16),
            jax.ShapeDtypeStruct((GROUP * columns, 128), jnp.bfloat16),
            jax.ShapeDtypeStruct((1, 1), jnp.float32),
        ),
        scratch_shapes=[
            pltpu.VMEM((2, kept, samples), jnp.float32),
            pltpu.VMEM((GROUP * columns, 128), jnp.float32),
        ],
        compiler_params=pltpu.CompilerParams(vmem_limit_bytes=32 * MIB),
        name="dft",
    )(freq_index.reshape(columns, Y), recorded.reshape(share * virtual, samples))
    spec = spec.reshape(columns, GROUP, 128)
    spec = lax.all_to_all(spec, "zx", split_axis=0, concat_axis=0, tiled=True)
    spec = lax.all_to_all(spec.transpose(1, 0, 2), COLUMN, split_axis=0, concat_axis=0, tiled=True)

    position = jnp.stack([y, core]).astype(jnp.int32)
    lines = 3 * columns + EXTRA
    vectors = pl.pallas_call(
        krylov_kernel,
        out_shape=jax.ShapeDtypeStruct((GROUP, lines, 128), jnp.bfloat16),
        in_specs=[pl.BlockSpec(memory_space=pltpu.SMEM)]
        + [pl.BlockSpec(memory_space=pltpu.VMEM)] * 2
        + [pl.BlockSpec(memory_space=pl.ANY)] * 8,
        out_specs=pl.BlockSpec(memory_space=pltpu.VMEM),
        scratch_shapes=[
            pltpu.VMEM((2 * sources, 8 * width), jnp.bfloat16),
            pltpu.VMEM((8 * columns, 128), jnp.float32),
            pltpu.VMEM((8 * width, 128), jnp.float32),
            pltpu.SemaphoreType.DMA((8,)),
        ],
        compiler_params=pltpu.CompilerParams(vmem_limit_bytes=32 * MIB),
        name="krylov",
    )(position, rec_norm, spec, *blocks)
    back = lax.all_to_all(vectors, COLUMN, split_axis=0, concat_axis=0, tiled=True)
    data = back[:, : 3 * columns].reshape(GROUP, 3, columns, 128).transpose(2, 0, 1, 3).reshape(columns, 24, 128)
    scal = jnp.sum(back[:, 3 * columns].astype(jnp.float32), axis=0).astype(jnp.bfloat16)
    scal = jnp.broadcast_to(scal, (columns, 2, 128))
    send = jnp.concatenate([data, scal], axis=1).reshape(columns, 13, 2, 128)
    got = lax.all_to_all(send, "zx", split_axis=0, concat_axis=0, tiled=True)
    got = got.reshape(columns, 26, 128).transpose(1, 0, 2)

    return pl.pallas_call(
        traces_kernel,
        out_shape=tuple(jax.ShapeDtypeStruct((share, virtual, samples), jnp.float32) for _ in range(2)),
        compiler_params=pltpu.CompilerParams(vmem_limit_bytes=32 * MIB),
        name="traces",
    )(got, table_hi, table_lo)


def solution(mesh):
    devices = mesh.devices
    fine = Mesh(devices.reshape(devices.shape[0] // 2, 2, devices.shape[1]), ("zx", "core", "rcv"))
    traces = P(("rcv", "zx", "core"), None, None)
    in_specs = (traces, P(("zx", "core"), None, None, "rcv"), P())
    return jax.shard_map(body, mesh=fine, in_specs=in_specs, out_specs=(traces, traces), check_vma=False)
```

```python
import functools
import math

import jax
import jax.numpy as jnp
from jax import lax
from jax.experimental import pallas as pl
from jax.experimental.pallas import tpu as pltpu
from jax.sharding import Mesh, PartitionSpec as P

X = 4
Y = 4
GROUP = 8
HV = 32
EXTRA = 16
HIGH = lax.Precision.HIGHEST
MIB = 1024 * 1024
COLUMN = ("core", "rcv")
SLAB = ("x", "core", "rcv")


def pick_kernel(idx_ref, k_ref, first_ref, second_ref, sems):
    upper = idx_ref[0] // 2
    copies = [
        pltpu.make_async_copy(k_ref.at[upper], first_ref, sems.at[0]),
        pltpu.make_async_copy(k_ref.at[1 - upper], second_ref, sems.at[1]),
    ]
    for copy in copies:
        copy.start()
    for copy in copies:
        copy.wait()


def angles(fr_ref, samples):
    unit = 2.0 * math.pi / samples
    fr = jnp.concatenate([fr_ref[:, n : n + 1] for n in range(fr_ref.shape[1])], axis=0)
    lane = lax.broadcasted_iota(jnp.int32, (fr.shape[0], 128), 1)
    fine = (fr * lane & (samples - 1)).astype(jnp.float32) * unit
    coarse = (fr * (lane * 128) & (samples - 1)).astype(jnp.float32) * unit
    factor = 1.0 / math.sqrt(samples)
    return jnp.cos(fine), jnp.sin(fine), jnp.cos(coarse) * factor, jnp.sin(coarse) * factor


def table_kernel(p, fr_ref, hi_ref, lo_ref):
    samples = hi_ref.shape[1]
    cos_f, sin_f, cos_c, sin_c = angles(fr_ref, samples)
    for a in range(samples // 128):
        ca, sa = cos_c[:, a : a + 1], sin_c[:, a : a + 1]
        part = slice(a * 128, (a + 1) * 128)
        value = ca * cos_f - sa * sin_f if p == 0 else -(sa * cos_f + ca * sin_f)
        top = value.astype(jnp.bfloat16)
        hi_ref[:, part] = top
        lo_ref[:, part] = (value - top.astype(jnp.float32)).astype(jnp.bfloat16)


def dft_kernel(fr_ref, rec_ref, out_ref, norm_ref, table, rows):
    deep = fr_ref.shape[0]
    samples = rec_ref.shape[1]
    cos_f, sin_f, cos_c, sin_c = angles(fr_ref, samples)
    for a in range(samples // 128):
        ca, sa = cos_c[:, a : a + 1], sin_c[:, a : a + 1]
        part = slice(a * 128, (a + 1) * 128)
        table[0, :, part] = ca * cos_f - sa * sin_f
        table[1, :, part] = -(sa * cos_f + ca * sin_f)
    rec = rec_ref[...]
    norm_ref[...] = jnp.sum(rec * rec, axis=(0, 1), keepdims=True)
    spec = [
        lax.dot_general(table[p], rec, (((1,), (1,)), ((), ())), precision=HIGH, preferred_element_type=jnp.float32)
        for p in range(2)
    ]
    for c in range(2):
        parts = [spec[p][:, (2 * src + c) * HV : (2 * src + c + 1) * HV] for src in range(2) for p in range(2)]
        both = jnp.concatenate(parts, axis=1)
        for x in range(X):
            for phi in range(Y):
                n = x * Y + phi
                start = x * GROUP + c * Y + phi
                rows[pl.ds(start, deep, stride=X * GROUP), :] = both[n * deep : (n + 1) * deep]
    out_ref[...] = rows[...].astype(jnp.bfloat16)


def quarter_turn(x):
    width = x.shape[1]
    even = lax.broadcasted_iota(jnp.int32, x.shape, 1) % 2 == 0
    return jnp.where(even, pltpu.roll(x, width - 1, 1), -pltpu.roll(x, 1, 1))


def total(x):
    return jnp.sum(x, axis=(0, 1), keepdims=True)


def length_of(x):
    return jnp.sqrt(total(x * x))


def inverse_of(x):
    return jnp.where(x > 1e-30, 1.0 / jnp.maximum(x, 1e-30), 0.0)


def krylov_kernel(idx_ref, norm_ref, u_ref, *refs):
    k_refs, g_ref = refs[:4], refs[4]
    u_rows, q_rows = refs[5:]
    deep = u_ref.shape[1]
    share = k_refs[0].shape[1]
    y, core = idx_ref[0], idx_ref[1]
    near = lax.rem(y, 2) * 2
    quarters = [(near if j % 2 == 0 else 2 - near) + (core if j < 2 else 1 - core) for j in range(4)]

    for x in range(X):
        for c in range(2):
            fields = [u_ref[x * GROUP + c * Y + ys].astype(jnp.float32) for ys in range(Y)]
            for g in range(4):
                both = jnp.concatenate([block[:, g * HV : (g + 1) * HV] for block in fields], axis=1)
                u_rows[pl.ds(x * 8 + c * 4 + g, deep, stride=8 * X), :] = both
    turned = u_rows[...].T
    u = jnp.concatenate([turned[ys * HV : (ys + 1) * HV] for ys in range(Y)], axis=1)

    def adjoint(p):
        both = jnp.concatenate([p, quarter_turn(p)], axis=0).astype(jnp.bfloat16)
        parts = [jnp.dot(both, k_ref[...], preferred_element_type=jnp.float32) for k_ref in k_refs]
        return 0.5 * jnp.concatenate(parts, axis=1)

    def forward(q):
        q = q.astype(jnp.bfloat16)
        w = sum(
            lax.dot_general(
                q[:, j * share : (j + 1) * share],
                k_refs[j][...],
                (((1,), (1,)), ((), ())),
                preferred_element_type=jnp.float32,
            )
            for j in range(4)
        )
        return 0.5 * (w[:HV] - quarter_turn(w[HV:]))

    length = length_of(u)
    scale = inverse_of(length)
    g1 = adjoint(u) * scale
    a1 = length_of(g1)
    q1 = g1 * inverse_of(a1)
    h2 = forward(q1) - (a1 * scale) * u
    b2 = length_of(h2)
    p2 = h2 * inverse_of(b2)
    g2 = adjoint(p2) - b2 * q1
    a2 = length_of(g2)
    q2 = g2 * inverse_of(a2)
    h3 = forward(q2) - a2 * p2
    b3 = length_of(h3)
    p3 = h3 * inverse_of(b3)
    g3 = adjoint(p3) - b3 * q2
    a3 = length_of(g3)
    q3 = g3 * inverse_of(a3)

    lane = lax.broadcasted_iota(jnp.int32, (EXTRA, 128), 1)
    slot = lax.rem(lane, 64) // GROUP
    values = jnp.zeros((EXTRA, 128), jnp.float32)
    for n, value in enumerate((math.sqrt(2.0) * length, a1, b2, a2, b3, a3, norm_ref[...])):
        values = jnp.where(slot == n, value, values)
    hi = values.astype(jnp.bfloat16).astype(jnp.float32)
    scalars = jnp.where(lane < 64, hi, values - hi)
    scalars = jnp.where(lax.rem(lane, GROUP) == core * Y + y, scalars, 0.0).astype(jnp.bfloat16)

    for pair in range(2):
        first, second = ((q1, q2), (q3, q3))[pair]
        q_rows[...] = jnp.concatenate([first, second], axis=0).T
        for x in range(X):
            for c in range(2):
                for j in range(4):
                    base = j * share + x * 4 + c * 2
                    even = q_rows[pl.ds(base, deep, stride=4 * X), :]
                    odd = q_rows[pl.ds(base + 1, deep, stride=4 * X), :]
                    for inner in range(2 - pair):
                        lanes = slice(inner * 64, (inner + 1) * 64)
                        both = jnp.concatenate([even[:, lanes], odd[:, lanes]], axis=1)
                        row = (2 * pair + inner) * deep
                        g_ref[x * GROUP + c * Y + quarters[j], row : row + deep, :] = both.astype(jnp.bfloat16)
    for e in range(X * GROUP):
        g_ref[e, 3 * deep : 3 * deep + EXTRA, :] = scalars


def reduced_lsqr(s, a1, b2, a2, b3, a3, rec):
    def norm(*parts):
        return jnp.sqrt(total(sum(part * part for part in parts)))

    beta = jnp.sqrt(total(rec))
    y11 = s / beta
    w1 = jnp.sqrt(jnp.maximum(1.0 - total(y11 * y11), 0.0))
    x = a1 * y11
    alpha = norm(x)
    x11 = x / alpha
    res, diag = beta, alpha
    y21, y22, w2 = a1 * x11 - alpha * y11, b2 * x11, -alpha * w1
    beta = jnp.sqrt(total(y21 * y21 + y22 * y22) + w2 * w2)
    y21, y22, w2 = y21 / beta, y22 / beta, w2 / beta
    x21, x22 = a1 * y21 + b2 * y22 - beta * x11, a2 * y22
    alpha = norm(x21, x22)
    x21, x22 = x21 / alpha, x22 / alpha

    def rotate(res, diag, beta, alpha):
        rho = jnp.sqrt(diag * diag + beta * beta)
        c, sn = diag / rho, beta / rho
        return c * res / rho, sn * alpha / rho, sn * res, -c * alpha

    step, couple, res, diag = rotate(res, diag, beta, alpha)
    sol1 = step * x11
    dir1, dir2 = x21 - couple * x11, x22
    y31, y32, y33 = a1 * x21 - alpha * y21, b2 * x21 + a2 * x22 - alpha * y22, b3 * x22
    w3 = -alpha * w2
    beta = jnp.sqrt(total(y31 * y31 + y32 * y32 + y33 * y33) + w3 * w3)
    y31, y32, y33 = y31 / beta, y32 / beta, y33 / beta
    x31 = a1 * y31 + b2 * y32 - beta * x21
    x32 = a2 * y32 + b3 * y33 - beta * x22
    x33 = a3 * y33
    alpha = norm(x31, x32, x33)
    step, couple, res, diag = rotate(res, diag, beta, alpha)
    last = res * diag / alpha
    return (sol1 + step * dir1, step * dir2), (last * x31, last * x32, last * x33)


def traces_kernel(m_ref, hi0_ref, lo0_ref, hi1_ref, lo1_ref, sol_ref, res_ref):
    scal = [m_ref[3 * X * GROUP + x].astype(jnp.float32) for x in range(X)]
    parts = []
    for n in range(7):
        top, low = n * GROUP, 64 + n * GROUP
        parts.append(
            jnp.concatenate([sc[:, top : top + GROUP] + sc[:, low : low + GROUP] for sc in scal], axis=1)
        )
    sol_c, res_c = reduced_lsqr(*parts)
    root = math.sqrt(2.0)
    sol_c, res_c = [root * w for w in sol_c], [root * w for w in res_c]
    lines = []
    for weights in (sol_c, res_c):
        for c in range(2):
            blocks = []
            for x in range(X):
                for phi in range(Y):
                    e = x * GROUP + c * Y + phi
                    blocks.append(
                        sum(w[:, e : e + 1] * m_ref[3 * e + n].astype(jnp.float32) for n, w in enumerate(weights))
                    )
            turned = jnp.concatenate(blocks, axis=0).T
            for rr in range(2):
                lines.append(
                    jnp.concatenate([turned[(2 * rr + q) * HV : (2 * rr + q + 1) * HV] for q in range(2)], axis=1)
                )
    rows = jnp.concatenate(lines, axis=0)
    hi = rows.astype(jnp.bfloat16)
    lo = (rows - hi.astype(jnp.float32)).astype(jnp.bfloat16)
    thi = jnp.concatenate([hi0_ref[...], hi1_ref[...]], axis=0)
    tlo = jnp.concatenate([lo0_ref[...], lo1_ref[...]], axis=0)

    def dot(a, b):
        return jnp.dot(a, b, preferred_element_type=jnp.float32)

    out = dot(hi, thi) + (dot(hi, tlo) + dot(lo, thi))
    for n, ref in enumerate((sol_ref, res_ref)):
        for c in range(2):
            for rr in range(2):
                row = ((n * 2 + c) * 2 + rr) * HV
                ref[rr, c * HV : (c + 1) * HV, :] = out[row : row + HV]


def body(recorded, kernel, freq_index):
    share, virtual, samples = recorded.shape
    kept = freq_index.shape[0]
    deep = kept // (X * Y)
    sources, local = kernel.shape[1], kernel.shape[3]
    core = lax.axis_index("core")
    y = lax.axis_index("rcv")
    position = jnp.stack([y, core]).astype(jnp.int32)
    anywhere = pl.BlockSpec(memory_space=pl.ANY)
    vmem = pl.BlockSpec(memory_space=pltpu.VMEM)
    smem = pl.BlockSpec(memory_space=pltpu.SMEM)
    limit = pltpu.CompilerParams(vmem_limit_bytes=32 * MIB)

    def route(flip):
        def target(c, here):
            return (here % 2) * Y + 2 * c + (here // 2 ^ flip)

        return [(c * Y + here, target(c, here)) for c in range(2) for here in range(Y)]

    payload = jax.ShapeDtypeStruct((2 * sources, local), jnp.bfloat16)
    loads = pl.pallas_call(
        pick_kernel,
        out_shape=(payload, payload),
        in_specs=[smem, anywhere],
        out_specs=(anywhere, anywhere),
        scratch_shapes=[pltpu.SemaphoreType.DMA((2,))],
        compiler_params=limit,
        name="pick",
    )(position, kernel.reshape(2, 2 * sources, local))
    blocks = [lax.ppermute(load, COLUMN, route(n)) for n, load in enumerate(loads)]
    def table(p, freqs):
        half = jax.ShapeDtypeStruct((kept, samples), jnp.bfloat16)
        return pl.pallas_call(
            functools.partial(table_kernel, p), out_shape=(half, half), compiler_params=limit, name=f"table{p}"
        )(freqs)

    freqs = freq_index.reshape(deep, X * Y)
    spec, rec_norm = pl.pallas_call(
        dft_kernel,
        out_shape=(
            jax.ShapeDtypeStruct((GROUP * X * deep, 128), jnp.bfloat16),
            jax.ShapeDtypeStruct((1, 1), jnp.float32),
        ),
        scratch_shapes=[
            pltpu.VMEM((2, kept, samples), jnp.float32),
            pltpu.VMEM((GROUP * X * deep, 128), jnp.float32),
        ],
        compiler_params=limit,
        name="dft",
    )(freqs, recorded.reshape(share * virtual, samples))

    spec, freqs = lax.optimization_barrier((spec, freqs))
    hi0, lo0 = table(0, freqs)
    spec = spec.reshape(deep, X * GROUP, 128)
    spec = lax.all_to_all(spec, "z", split_axis=0, concat_axis=0, tiled=True)
    spec, freqs, *blocks = lax.optimization_barrier((spec, freqs, *blocks))
    hi1, lo1 = table(1, freqs)
    blocks = blocks + [lax.ppermute(b, "core", [(0, 1), (1, 0)]) for b in blocks]
    spec = lax.all_to_all(spec.transpose(1, 0, 2), SLAB, split_axis=0, concat_axis=0, tiled=True)

    lines = 3 * deep + EXTRA
    vectors = pl.pallas_call(
        krylov_kernel,
        out_shape=jax.ShapeDtypeStruct((X * GROUP, lines, 128), jnp.bfloat16),
        in_specs=[smem] + [vmem] * 6,
        out_specs=vmem,
        scratch_shapes=[
            pltpu.VMEM((8 * X * deep, 128), jnp.float32),
            pltpu.VMEM((4 * local, 128), jnp.float32),
        ],
        compiler_params=limit,
        name="krylov",
    )(position, rec_norm, spec, *blocks)
    back = lax.all_to_all(vectors, SLAB, split_axis=0, concat_axis=0, tiled=True)
    data = back[:, : 3 * deep].reshape(X * GROUP, 3, deep, 128).transpose(2, 0, 1, 3)
    data = data.reshape(deep, 3 * X * GROUP, 128)
    scal = back[:, 3 * deep].astype(jnp.float32).reshape(X, GROUP, 128)
    scal = jnp.sum(scal, axis=1).astype(jnp.bfloat16)
    scal = jnp.concatenate([scal, jnp.zeros_like(scal)], axis=0)
    send = jnp.concatenate([data, jnp.broadcast_to(scal, (deep, 2 * X, 128))], axis=1)
    got = lax.all_to_all(send, "z", split_axis=0, concat_axis=0, tiled=True).transpose(1, 0, 2)

    return pl.pallas_call(
        traces_kernel,
        out_shape=tuple(jax.ShapeDtypeStruct((share, virtual, samples), jnp.float32) for _ in range(2)),
        compiler_params=limit,
        name="traces",
    )(got, hi0, lo0, hi1, lo1)


def solution(mesh):
    devices = mesh.devices
    deep = devices.shape[0] // (2 * X)
    fine = Mesh(devices.reshape(deep, X, 2, devices.shape[1]), ("z", "x", "core", "rcv"))
    traces = P(("rcv", "z", "x", "core"), None, None)
    in_specs = (traces, P(("z", "x", "core"), None, None, "rcv"), P())
    return jax.shard_map(body, mesh=fine, in_specs=in_specs, out_specs=(traces, traces), check_vma=False)
```

```python
import functools
import math

import jax
import jax.numpy as jnp
from jax import lax
from jax.experimental import pallas as pl
from jax.experimental.pallas import tpu as pltpu
from jax.sharding import Mesh, PartitionSpec as P

X = 4
Y = 4
GROUP = 8
HV = 32
EXTRA = 16
HIGH = lax.Precision.HIGHEST
MIB = 1024 * 1024
COLUMN = ("core", "rcv")
SLAB = ("x", "core", "rcv")


def pick_kernel(idx_ref, k_ref, first_ref, second_ref, sems):
    upper = idx_ref[0] // 2
    copies = [
        pltpu.make_async_copy(k_ref.at[upper], first_ref, sems.at[0]),
        pltpu.make_async_copy(k_ref.at[1 - upper], second_ref, sems.at[1]),
    ]
    for copy in copies:
        copy.start()
    for copy in copies:
        copy.wait()


def angles(fr_ref, samples):
    unit = 2.0 * math.pi / samples
    fr = jnp.concatenate([fr_ref[:, n : n + 1] for n in range(fr_ref.shape[1])], axis=0)
    lane = lax.broadcasted_iota(jnp.int32, (fr.shape[0], 128), 1)
    fine = (fr * lane & (samples - 1)).astype(jnp.float32) * unit
    coarse = (fr * (lane * 128) & (samples - 1)).astype(jnp.float32) * unit
    factor = 1.0 / math.sqrt(samples)
    return jnp.cos(fine), jnp.sin(fine), jnp.cos(coarse) * factor, jnp.sin(coarse) * factor


def table_kernel(p, fr_ref, hi_ref, lo_ref):
    samples = hi_ref.shape[1]
    cos_f, sin_f, cos_c, sin_c = angles(fr_ref, samples)
    for a in range(samples // 128):
        ca, sa = cos_c[:, a : a + 1], sin_c[:, a : a + 1]
        part = slice(a * 128, (a + 1) * 128)
        value = ca * cos_f - sa * sin_f if p == 0 else -(sa * cos_f + ca * sin_f)
        top = value.astype(jnp.bfloat16)
        hi_ref[:, part] = top
        lo_ref[:, part] = (value - top.astype(jnp.float32)).astype(jnp.bfloat16)


def dft_kernel(fr_ref, rec_ref, out_ref, norm_ref, table, rows):
    deep = fr_ref.shape[0]
    samples = rec_ref.shape[1]
    cos_f, sin_f, cos_c, sin_c = angles(fr_ref, samples)
    for a in range(samples // 128):
        ca, sa = cos_c[:, a : a + 1], sin_c[:, a : a + 1]
        part = slice(a * 128, (a + 1) * 128)
        table[0, :, part] = ca * cos_f - sa * sin_f
        table[1, :, part] = -(sa * cos_f + ca * sin_f)
    rec = rec_ref[...]
    norm_ref[...] = jnp.sum(rec * rec, axis=(0, 1), keepdims=True)
    spec = [
        lax.dot_general(table[p], rec, (((1,), (1,)), ((), ())), precision=HIGH, preferred_element_type=jnp.float32)
        for p in range(2)
    ]
    for c in range(2):
        parts = [spec[p][:, (2 * src + c) * HV : (2 * src + c + 1) * HV] for src in range(2) for p in range(2)]
        both = jnp.concatenate(parts, axis=1)
        for x in range(X):
            for phi in range(Y):
                n = x * Y + phi
                start = x * GROUP + c * Y + phi
                rows[pl.ds(start, deep, stride=X * GROUP), :] = both[n * deep : (n + 1) * deep]
    out_ref[...] = rows[...].astype(jnp.bfloat16)


def quarter_turn(x):
    width = x.shape[1]
    even = lax.broadcasted_iota(jnp.int32, x.shape, 1) % 2 == 0
    return jnp.where(even, pltpu.roll(x, width - 1, 1), -pltpu.roll(x, 1, 1))


def total(x):
    return jnp.sum(x, axis=(0, 1), keepdims=True)


def length_of(x):
    return jnp.sqrt(total(x * x))


def inverse_of(x):
    return jnp.where(x > 1e-30, 1.0 / jnp.maximum(x, 1e-30), 0.0)


def apply_adjoint(p, k_refs):
    both = jnp.concatenate([p, quarter_turn(p)], axis=0).astype(jnp.bfloat16)
    depth = both.shape[1] // 2
    parts = [jnp.dot(both, k_ref[...], preferred_element_type=jnp.float32) for k_ref in k_refs[:2]]
    for top, low in (k_refs[2:4], k_refs[4:6]):
        parts.append(
            jnp.dot(both[:, :depth], top[...], preferred_element_type=jnp.float32)
            + jnp.dot(both[:, depth:], low[...], preferred_element_type=jnp.float32)
        )
    return 0.5 * jnp.concatenate(parts, axis=1)


def apply_forward(q, k_refs):
    q = q.astype(jnp.bfloat16)
    share = k_refs[0].shape[1]

    def product(j, k_ref):
        part = q[:, j * share : (j + 1) * share]
        return lax.dot_general(part, k_ref[...], (((1,), (1,)), ((), ())), preferred_element_type=jnp.float32)

    w = product(0, k_refs[0]) + product(1, k_refs[1])
    tops = product(2, k_refs[2]) + product(3, k_refs[4])
    lows = product(2, k_refs[3]) + product(3, k_refs[5])
    w = w + jnp.concatenate([tops, lows], axis=1)
    return 0.5 * (w[:HV] - quarter_turn(w[HV:]))


def fill(row, entries):
    slot = lax.rem(lax.broadcasted_iota(jnp.int32, row.shape, 1), 64) // GROUP
    for n, value in entries:
        row = jnp.where(slot == n, value, row)
    return row


def write_vectors(idx_ref, q_rows, first, second, count, g_ref, deep):
    y, core = idx_ref[0], idx_ref[1]
    near = lax.rem(y, 2) * 2
    quarters = [(near if j % 2 == 0 else 2 - near) + (core if j < 2 else 1 - core) for j in range(4)]
    share = first.shape[1] // 4
    q_rows[...] = jnp.concatenate([first, second], axis=0).T
    for x in range(X):
        for c in range(2):
            for j in range(4):
                base = j * share + x * 4 + c * 2
                even = q_rows[pl.ds(base, deep, stride=4 * X), :]
                odd = q_rows[pl.ds(base + 1, deep, stride=4 * X), :]
                for n in range(count):
                    lanes = slice(n * 64, (n + 1) * 64)
                    both = jnp.concatenate([even[:, lanes], odd[:, lanes]], axis=1)
                    g_ref[x * GROUP + c * Y + quarters[j], n * deep : (n + 1) * deep, :] = both.astype(jnp.bfloat16)


def krylov_first_kernel(idx_ref, norm_ref, u_ref, *refs):
    k_refs = refs[:6]
    g_ref, p_ref, q_ref, a_ref, row_ref, u_rows, q_rows = refs[6:]
    deep = u_ref.shape[1]
    for x in range(X):
        for c in range(2):
            fields = [u_ref[x * GROUP + c * Y + ys].astype(jnp.float32) for ys in range(Y)]
            for g in range(4):
                both = jnp.concatenate([block[:, g * HV : (g + 1) * HV] for block in fields], axis=1)
                u_rows[pl.ds(x * 8 + c * 4 + g, deep, stride=8 * X), :] = both
    turned = u_rows[...].T
    u = jnp.concatenate([turned[ys * HV : (ys + 1) * HV] for ys in range(Y)], axis=1)

    length = length_of(u)
    scale = inverse_of(length)
    g1 = apply_adjoint(u, k_refs) * scale
    a1 = length_of(g1)
    q1 = g1 * inverse_of(a1)
    h2 = apply_forward(q1, k_refs) - (a1 * scale) * u
    b2 = length_of(h2)
    p2 = h2 * inverse_of(b2)
    g2 = apply_adjoint(p2, k_refs) - b2 * q1
    a2 = length_of(g2)
    q2 = g2 * inverse_of(a2)
    p_ref[...] = p2
    q_ref[...] = q2
    a_ref[...] = a2
    entries = ((0, math.sqrt(2.0) * length), (1, a1), (2, b2), (3, a2), (6, norm_ref[...]))
    row_ref[...] = fill(jnp.zeros((EXTRA, 128), jnp.float32), entries)
    write_vectors(idx_ref, q_rows, q1, q2, 2, g_ref, deep)


def krylov_second_kernel(idx_ref, p_ref, q_ref, a_ref, row_ref, *refs):
    k_refs = refs[:6]
    g_ref, q_rows = refs[6:]
    deep = g_ref.shape[1] - EXTRA
    q2 = q_ref[...]
    h3 = apply_forward(q2, k_refs) - a_ref[...] * p_ref[...]
    b3 = length_of(h3)
    p3 = h3 * inverse_of(b3)
    g3 = apply_adjoint(p3, k_refs) - b3 * q2
    a3 = length_of(g3)
    q3 = g3 * inverse_of(a3)
    values = fill(row_ref[...], ((4, b3), (5, a3)))
    lane = lax.broadcasted_iota(jnp.int32, (EXTRA, 128), 1)
    hi = values.astype(jnp.bfloat16).astype(jnp.float32)
    scalars = jnp.where(lane < 64, hi, values - hi)
    mine = idx_ref[1] * Y + idx_ref[0]
    scalars = jnp.where(lax.rem(lane, GROUP) == mine, scalars, 0.0).astype(jnp.bfloat16)
    write_vectors(idx_ref, q_rows, q3, q3, 1, g_ref, deep)
    for e in range(X * GROUP):
        g_ref[e, deep : deep + EXTRA, :] = scalars


def reduced_lsqr(s, a1, b2, a2, b3, a3, rec):
    def norm(*parts):
        return jnp.sqrt(total(sum(part * part for part in parts)))

    beta = jnp.sqrt(total(rec))
    y11 = s / beta
    w1 = jnp.sqrt(jnp.maximum(1.0 - total(y11 * y11), 0.0))
    x = a1 * y11
    alpha = norm(x)
    x11 = x / alpha
    res, diag = beta, alpha
    y21, y22, w2 = a1 * x11 - alpha * y11, b2 * x11, -alpha * w1
    beta = jnp.sqrt(total(y21 * y21 + y22 * y22) + w2 * w2)
    y21, y22, w2 = y21 / beta, y22 / beta, w2 / beta
    x21, x22 = a1 * y21 + b2 * y22 - beta * x11, a2 * y22
    alpha = norm(x21, x22)
    x21, x22 = x21 / alpha, x22 / alpha

    def rotate(res, diag, beta, alpha):
        rho = jnp.sqrt(diag * diag + beta * beta)
        c, sn = diag / rho, beta / rho
        return c * res / rho, sn * alpha / rho, sn * res, -c * alpha

    step, couple, res, diag = rotate(res, diag, beta, alpha)
    sol1 = step * x11
    dir1, dir2 = x21 - couple * x11, x22
    y31, y32, y33 = a1 * x21 - alpha * y21, b2 * x21 + a2 * x22 - alpha * y22, b3 * x22
    w3 = -alpha * w2
    beta = jnp.sqrt(total(y31 * y31 + y32 * y32 + y33 * y33) + w3 * w3)
    y31, y32, y33 = y31 / beta, y32 / beta, y33 / beta
    x31 = a1 * y31 + b2 * y32 - beta * x21
    x32 = a2 * y32 + b3 * y33 - beta * x22
    x33 = a3 * y33
    alpha = norm(x31, x32, x33)
    step, couple, res, diag = rotate(res, diag, beta, alpha)
    last = res * diag / alpha
    return (sol1 + step * dir1, step * dir2), (last * x31, last * x32, last * x33)


def traces_kernel(m_ref, last_ref, hi0_ref, lo0_ref, hi1_ref, lo1_ref, sol_ref, res_ref):
    scal = [last_ref[X * GROUP + x].astype(jnp.float32) for x in range(X)]
    parts = []
    for n in range(7):
        top, low = n * GROUP, 64 + n * GROUP
        parts.append(
            jnp.concatenate([sc[:, top : top + GROUP] + sc[:, low : low + GROUP] for sc in scal], axis=1)
        )
    sol_c, res_c = reduced_lsqr(*parts)
    root = math.sqrt(2.0)
    sol_c, res_c = [root * w for w in sol_c], [root * w for w in res_c]
    lines = []
    for weights in (sol_c, res_c):
        for c in range(2):
            blocks = []
            for x in range(X):
                for phi in range(Y):
                    e = x * GROUP + c * Y + phi
                    block = sum(
                        w[:, e : e + 1] * m_ref[2 * e + n].astype(jnp.float32) for n, w in enumerate(weights[:2])
                    )
                    for w in weights[2:]:
                        block = block + w[:, e : e + 1] * last_ref[e].astype(jnp.float32)
                    blocks.append(block)
            turned = jnp.concatenate(blocks, axis=0).T
            for rr in range(2):
                lines.append(
                    jnp.concatenate([turned[(2 * rr + q) * HV : (2 * rr + q + 1) * HV] for q in range(2)], axis=1)
                )
    rows = jnp.concatenate(lines, axis=0)
    hi = rows.astype(jnp.bfloat16)
    lo = (rows - hi.astype(jnp.float32)).astype(jnp.bfloat16)
    thi = jnp.concatenate([hi0_ref[...], hi1_ref[...]], axis=0)
    tlo = jnp.concatenate([lo0_ref[...], lo1_ref[...]], axis=0)

    def dot(a, b):
        return jnp.dot(a, b, preferred_element_type=jnp.float32)

    out = dot(hi, thi) + (dot(hi, tlo) + dot(lo, thi))
    for n, ref in enumerate((sol_ref, res_ref)):
        for c in range(2):
            for rr in range(2):
                row = ((n * 2 + c) * 2 + rr) * HV
                ref[rr, c * HV : (c + 1) * HV, :] = out[row : row + HV]


def body(recorded, kernel, freq_index):
    share, virtual, samples = recorded.shape
    kept = freq_index.shape[0]
    deep = kept // (X * Y)
    sources, local = kernel.shape[1], kernel.shape[3]
    core = lax.axis_index("core")
    y = lax.axis_index("rcv")
    position = jnp.stack([y, core]).astype(jnp.int32)
    anywhere = pl.BlockSpec(memory_space=pl.ANY)
    vmem = pl.BlockSpec(memory_space=pltpu.VMEM)
    smem = pl.BlockSpec(memory_space=pltpu.SMEM)
    limit = pltpu.CompilerParams(vmem_limit_bytes=32 * MIB)

    def route(flip):
        def target(c, here):
            return (here % 2) * Y + 2 * c + (here // 2 ^ flip)

        return [(c * Y + here, target(c, here)) for c in range(2) for here in range(Y)]

    payload = jax.ShapeDtypeStruct((2 * sources, local), jnp.bfloat16)
    loads = pl.pallas_call(
        pick_kernel,
        out_shape=(payload, payload),
        in_specs=[smem, anywhere],
        out_specs=(anywhere, anywhere),
        scratch_shapes=[pltpu.SemaphoreType.DMA((2,))],
        compiler_params=limit,
        name="pick",
    )(position, kernel.reshape(2, 2 * sources, local))
    blocks = [lax.ppermute(load, COLUMN, route(n)) for n, load in enumerate(loads)]
    def table(p, freqs):
        half = jax.ShapeDtypeStruct((kept, samples), jnp.bfloat16)
        return pl.pallas_call(
            functools.partial(table_kernel, p), out_shape=(half, half), compiler_params=limit, name=f"table{p}"
        )(freqs)

    freqs = freq_index.reshape(deep, X * Y)
    spec, rec_norm = pl.pallas_call(
        dft_kernel,
        out_shape=(
            jax.ShapeDtypeStruct((GROUP * X * deep, 128), jnp.bfloat16),
            jax.ShapeDtypeStruct((1, 1), jnp.float32),
        ),
        scratch_shapes=[
            pltpu.VMEM((2, kept, samples), jnp.float32),
            pltpu.VMEM((GROUP * X * deep, 128), jnp.float32),
        ],
        compiler_params=limit,
        name="dft",
    )(freqs, recorded.reshape(share * virtual, samples))

    spec, freqs, *blocks = lax.optimization_barrier((spec, freqs, *blocks))
    hi0, lo0 = table(0, freqs)
    hi1, lo1 = table(1, freqs)
    for b in blocks[:2]:
        halves = b[:sources], b[sources:]
        blocks = blocks + [lax.ppermute(half, "core", [(0, 1), (1, 0)]) for half in halves]
    spec = spec.reshape(deep, X * GROUP, 128)
    spec = lax.all_to_all(spec, "z", split_axis=0, concat_axis=0, tiled=True)
    spec = lax.all_to_all(spec.transpose(1, 0, 2), SLAB, split_axis=0, concat_axis=0, tiled=True)

    slab = X * GROUP
    q_rows = pltpu.VMEM((4 * local, 128), jnp.float32)
    single = jax.ShapeDtypeStruct((1, 1), jnp.float32)
    row = jax.ShapeDtypeStruct((EXTRA, 128), jnp.float32)
    pair, *state = pl.pallas_call(
        krylov_first_kernel,
        out_shape=(
            jax.ShapeDtypeStruct((slab, 2 * deep, 128), jnp.bfloat16),
            jax.ShapeDtypeStruct((HV, 2 * sources), jnp.float32),
            jax.ShapeDtypeStruct((2 * HV, 4 * local), jnp.float32),
            single,
            row,
        ),
        in_specs=[smem] + [vmem] * 8,
        out_specs=(vmem,) * 5,
        scratch_shapes=[pltpu.VMEM((8 * slab * deep // GROUP, 128), jnp.float32), q_rows],
        compiler_params=limit,
        name="krylov_first",
    )(position, rec_norm, spec, *blocks)
    pair = lax.all_to_all(pair, SLAB, split_axis=0, concat_axis=0, tiled=True)
    pair = pair.reshape(slab, 2, deep, 128).transpose(2, 0, 1, 3).reshape(deep, 2 * slab, 128)

    last = pl.pallas_call(
        krylov_second_kernel,
        out_shape=jax.ShapeDtypeStruct((slab, deep + EXTRA, 128), jnp.bfloat16),
        in_specs=[smem] + [vmem] * 10,
        out_specs=vmem,
        scratch_shapes=[q_rows],
        compiler_params=limit,
        cost_estimate=pl.CostEstimate(
            flops=8 * HV * 2 * sources * 4 * local, bytes_accessed=16 * sources * local, transcendentals=0
        ),
        name="krylov_second",
    )(position, *state, *blocks)
    last = lax.all_to_all(last, SLAB, split_axis=0, concat_axis=0, tiled=True)
    scal = last[:, deep].astype(jnp.float32).reshape(X, GROUP, 128)
    scal = jnp.sum(scal, axis=1).astype(jnp.bfloat16)
    scal = jnp.concatenate([scal, jnp.zeros((8 - X, 128), jnp.bfloat16)], axis=0)
    last = jnp.concatenate([last[:, :deep].transpose(1, 0, 2), jnp.broadcast_to(scal, (deep, 8, 128))], axis=1)

    pair = lax.all_to_all(pair, "z", split_axis=0, concat_axis=0, tiled=True).transpose(1, 0, 2)
    last = lax.all_to_all(last, "z", split_axis=0, concat_axis=0, tiled=True).transpose(1, 0, 2)
    return pl.pallas_call(
        traces_kernel,
        out_shape=tuple(jax.ShapeDtypeStruct((share, virtual, samples), jnp.float32) for _ in range(2)),
        compiler_params=limit,
        name="traces",
    )(pair, last, hi0, lo0, hi1, lo1)


def solution(mesh):
    devices = mesh.devices
    deep = devices.shape[0] // (2 * X)
    fine = Mesh(devices.reshape(deep, X, 2, devices.shape[1]), ("z", "x", "core", "rcv"))
    traces = P(("rcv", "z", "x", "core"), None, None)
    in_specs = (traces, P(("z", "x", "core"), None, None, "rcv"), P())
    return jax.shard_map(body, mesh=fine, in_specs=in_specs, out_specs=(traces, traces), check_vma=False)
```

```python
import functools
import math

import jax
import jax.numpy as jnp
from jax import lax
from jax.experimental import pallas as pl
from jax.experimental.pallas import tpu as pltpu
from jax.sharding import Mesh, PartitionSpec as P

X = 4
Y = 4
GROUP = 8
HV = 32
EXTRA = 16
HIGH = lax.Precision.HIGHEST
MIB = 1024 * 1024
COLUMN = ("core", "rcv")
SLAB = ("x", "core", "rcv")


def pick_kernel(idx_ref, k_ref, first_ref, second_ref, sems):
    upper = idx_ref[0] // 2
    copies = [
        pltpu.make_async_copy(k_ref.at[upper], first_ref, sems.at[0]),
        pltpu.make_async_copy(k_ref.at[1 - upper], second_ref, sems.at[1]),
    ]
    for copy in copies:
        copy.start()
    for copy in copies:
        copy.wait()


def angles(fr_ref, samples):
    unit = 2.0 * math.pi / samples
    fr = jnp.concatenate([fr_ref[:, n : n + 1] for n in range(fr_ref.shape[1])], axis=0)
    lane = lax.broadcasted_iota(jnp.int32, (fr.shape[0], 128), 1)
    fine = (fr * lane & (samples - 1)).astype(jnp.float32) * unit
    coarse = (fr * (lane * 128) & (samples - 1)).astype(jnp.float32) * unit
    factor = 1.0 / math.sqrt(samples)
    return jnp.cos(fine), jnp.sin(fine), jnp.cos(coarse) * factor, jnp.sin(coarse) * factor


def table_kernel(p, fr_ref, hi_ref, lo_ref):
    samples = hi_ref.shape[1]
    cos_f, sin_f, cos_c, sin_c = angles(fr_ref, samples)
    for a in range(samples // 128):
        ca, sa = cos_c[:, a : a + 1], sin_c[:, a : a + 1]
        part = slice(a * 128, (a + 1) * 128)
        value = ca * cos_f - sa * sin_f if p == 0 else -(sa * cos_f + ca * sin_f)
        top = value.astype(jnp.bfloat16)
        hi_ref[:, part] = top
        lo_ref[:, part] = (value - top.astype(jnp.float32)).astype(jnp.bfloat16)


def dft_kernel(fr_ref, rec_ref, out_ref, norm_ref, table, rows):
    deep = fr_ref.shape[0]
    samples = rec_ref.shape[1]
    cos_f, sin_f, cos_c, sin_c = angles(fr_ref, samples)
    for a in range(samples // 128):
        ca, sa = cos_c[:, a : a + 1], sin_c[:, a : a + 1]
        part = slice(a * 128, (a + 1) * 128)
        table[0, :, part] = ca * cos_f - sa * sin_f
        table[1, :, part] = -(sa * cos_f + ca * sin_f)
    rec = rec_ref[...]
    norm_ref[...] = jnp.sum(rec * rec, axis=(0, 1), keepdims=True)
    spec = [
        lax.dot_general(table[p], rec, (((1,), (1,)), ((), ())), precision=HIGH, preferred_element_type=jnp.float32)
        for p in range(2)
    ]
    for c in range(2):
        parts = [spec[p][:, (2 * src + c) * HV : (2 * src + c + 1) * HV] for src in range(2) for p in range(2)]
        both = jnp.concatenate(parts, axis=1)
        for x in range(X):
            for phi in range(Y):
                n = x * Y + phi
                start = x * GROUP + c * Y + phi
                rows[pl.ds(start, deep, stride=X * GROUP), :] = both[n * deep : (n + 1) * deep]
    out_ref[...] = rows[...].astype(jnp.bfloat16)


def quarter_turn(x):
    width = x.shape[1]
    even = lax.broadcasted_iota(jnp.int32, x.shape, 1) % 2 == 0
    return jnp.where(even, pltpu.roll(x, width - 1, 1), -pltpu.roll(x, 1, 1))


def total(x):
    return jnp.sum(x, axis=(0, 1), keepdims=True)


def length_of(x):
    return jnp.sqrt(total(x * x))


def inverse_of(x):
    return jnp.where(x > 1e-30, 1.0 / jnp.maximum(x, 1e-30), 0.0)


def gather_kernel(u_ref, out_ref, u_rows):
    deep = u_ref.shape[1]
    for x in range(X):
        for c in range(2):
            fields = [u_ref[x * GROUP + c * Y + ys].astype(jnp.float32) for ys in range(Y)]
            for g in range(4):
                both = jnp.concatenate([block[:, g * HV : (g + 1) * HV] for block in fields], axis=1)
                u_rows[pl.ds(x * 8 + c * 4 + g, deep, stride=8 * X), :] = both
    turned = u_rows[...].T
    out_ref[...] = jnp.concatenate([turned[ys * HV : (ys + 1) * HV] for ys in range(Y)], axis=1)


def krylov_kernel(idx_ref, norm_ref, u_ref, *refs):
    k_refs, g_ref = refs[:4], refs[4]
    (q_rows,) = refs[5:]
    deep = (g_ref.shape[1] - EXTRA) // 3
    share = k_refs[0].shape[1]
    y, core = idx_ref[0], idx_ref[1]
    near = lax.rem(y, 2) * 2
    quarters = [(near if j % 2 == 0 else 2 - near) + (core if j < 2 else 1 - core) for j in range(4)]

    u = u_ref[...]

    def adjoint(p):
        both = jnp.concatenate([p, quarter_turn(p)], axis=0).astype(jnp.bfloat16)
        parts = [jnp.dot(both, k_ref[...], preferred_element_type=jnp.float32) for k_ref in k_refs]
        return 0.5 * jnp.concatenate(parts, axis=1)

    def forward(q):
        q = q.astype(jnp.bfloat16)
        w = sum(
            lax.dot_general(
                q[:, j * share : (j + 1) * share],
                k_refs[j][...],
                (((1,), (1,)), ((), ())),
                preferred_element_type=jnp.float32,
            )
            for j in range(4)
        )
        return 0.5 * (w[:HV] - quarter_turn(w[HV:]))

    length = length_of(u)
    scale = inverse_of(length)
    g1 = adjoint(u) * scale
    a1 = length_of(g1)
    q1 = g1 * inverse_of(a1)
    h2 = forward(q1) - (a1 * scale) * u
    b2 = length_of(h2)
    p2 = h2 * inverse_of(b2)
    g2 = adjoint(p2) - b2 * q1
    a2 = length_of(g2)
    q2 = g2 * inverse_of(a2)
    h3 = forward(q2) - a2 * p2
    b3 = length_of(h3)
    p3 = h3 * inverse_of(b3)
    g3 = adjoint(p3) - b3 * q2
    a3 = length_of(g3)
    q3 = g3 * inverse_of(a3)

    lane = lax.broadcasted_iota(jnp.int32, (EXTRA, 128), 1)
    slot = lax.rem(lane, 64) // GROUP
    values = jnp.zeros((EXTRA, 128), jnp.float32)
    for n, value in enumerate((math.sqrt(2.0) * length, a1, b2, a2, b3, a3, norm_ref[...])):
        values = jnp.where(slot == n, value, values)
    hi = values.astype(jnp.bfloat16).astype(jnp.float32)
    scalars = jnp.where(lane < 64, hi, values - hi)
    scalars = jnp.where(lax.rem(lane, GROUP) == core * Y + y, scalars, 0.0).astype(jnp.bfloat16)

    for pair in range(2):
        first, second = ((q1, q2), (q3, q3))[pair]
        q_rows[...] = jnp.concatenate([first, second], axis=0).T
        for x in range(X):
            for c in range(2):
                for j in range(4):
                    base = j * share + x * 4 + c * 2
                    even = q_rows[pl.ds(base, deep, stride=4 * X), :]
                    odd = q_rows[pl.ds(base + 1, deep, stride=4 * X), :]
                    for inner in range(2 - pair):
                        lanes = slice(inner * 64, (inner + 1) * 64)
                        both = jnp.concatenate([even[:, lanes], odd[:, lanes]], axis=1)
                        row = (2 * pair + inner) * deep
                        g_ref[x * GROUP + c * Y + quarters[j], row : row + deep, :] = both.astype(jnp.bfloat16)
    for e in range(X * GROUP):
        g_ref[e, 3 * deep : 3 * deep + EXTRA, :] = scalars


def reduced_lsqr(s, a1, b2, a2, b3, a3, rec):
    def norm(*parts):
        return jnp.sqrt(total(sum(part * part for part in parts)))

    beta = jnp.sqrt(total(rec))
    y11 = s / beta
    w1 = jnp.sqrt(jnp.maximum(1.0 - total(y11 * y11), 0.0))
    x = a1 * y11
    alpha = norm(x)
    x11 = x / alpha
    res, diag = beta, alpha
    y21, y22, w2 = a1 * x11 - alpha * y11, b2 * x11, -alpha * w1
    beta = jnp.sqrt(total(y21 * y21 + y22 * y22) + w2 * w2)
    y21, y22, w2 = y21 / beta, y22 / beta, w2 / beta
    x21, x22 = a1 * y21 + b2 * y22 - beta * x11, a2 * y22
    alpha = norm(x21, x22)
    x21, x22 = x21 / alpha, x22 / alpha

    def rotate(res, diag, beta, alpha):
        rho = jnp.sqrt(diag * diag + beta * beta)
        c, sn = diag / rho, beta / rho
        return c * res / rho, sn * alpha / rho, sn * res, -c * alpha

    step, couple, res, diag = rotate(res, diag, beta, alpha)
    sol1 = step * x11
    dir1, dir2 = x21 - couple * x11, x22
    y31, y32, y33 = a1 * x21 - alpha * y21, b2 * x21 + a2 * x22 - alpha * y22, b3 * x22
    w3 = -alpha * w2
    beta = jnp.sqrt(total(y31 * y31 + y32 * y32 + y33 * y33) + w3 * w3)
    y31, y32, y33 = y31 / beta, y32 / beta, y33 / beta
    x31 = a1 * y31 + b2 * y32 - beta * x21
    x32 = a2 * y32 + b3 * y33 - beta * x22
    x33 = a3 * y33
    alpha = norm(x31, x32, x33)
    step, couple, res, diag = rotate(res, diag, beta, alpha)
    last = res * diag / alpha
    return (sol1 + step * dir1, step * dir2), (last * x31, last * x32, last * x33)


def traces_kernel(m_ref, hi0_ref, lo0_ref, hi1_ref, lo1_ref, sol_ref, res_ref):
    scal = [m_ref[3 * X * GROUP + x].astype(jnp.float32) for x in range(X)]
    parts = []
    for n in range(7):
        top, low = n * GROUP, 64 + n * GROUP
        parts.append(
            jnp.concatenate([sc[:, top : top + GROUP] + sc[:, low : low + GROUP] for sc in scal], axis=1)
        )
    sol_c, res_c = reduced_lsqr(*parts)
    root = math.sqrt(2.0)
    sol_c, res_c = [root * w for w in sol_c], [root * w for w in res_c]
    lines = []
    for weights in (sol_c, res_c):
        for c in range(2):
            blocks = []
            for x in range(X):
                for phi in range(Y):
                    e = x * GROUP + c * Y + phi
                    blocks.append(
                        sum(w[:, e : e + 1] * m_ref[3 * e + n].astype(jnp.float32) for n, w in enumerate(weights))
                    )
            turned = jnp.concatenate(blocks, axis=0).T
            for rr in range(2):
                lines.append(
                    jnp.concatenate([turned[(2 * rr + q) * HV : (2 * rr + q + 1) * HV] for q in range(2)], axis=1)
                )
    rows = jnp.concatenate(lines, axis=0)
    hi = rows.astype(jnp.bfloat16)
    lo = (rows - hi.astype(jnp.float32)).astype(jnp.bfloat16)
    thi = jnp.concatenate([hi0_ref[...], hi1_ref[...]], axis=0)
    tlo = jnp.concatenate([lo0_ref[...], lo1_ref[...]], axis=0)

    def dot(a, b):
        return jnp.dot(a, b, preferred_element_type=jnp.float32)

    out = dot(hi, thi) + (dot(hi, tlo) + dot(lo, thi))
    for n, ref in enumerate((sol_ref, res_ref)):
        for c in range(2):
            for rr in range(2):
                row = ((n * 2 + c) * 2 + rr) * HV
                ref[rr, c * HV : (c + 1) * HV, :] = out[row : row + HV]


def body(recorded, kernel, freq_index):
    share, virtual, samples = recorded.shape
    kept = freq_index.shape[0]
    deep = kept // (X * Y)
    sources, local = kernel.shape[1], kernel.shape[3]
    core = lax.axis_index("core")
    y = lax.axis_index("rcv")
    position = jnp.stack([y, core]).astype(jnp.int32)
    anywhere = pl.BlockSpec(memory_space=pl.ANY)
    vmem = pl.BlockSpec(memory_space=pltpu.VMEM)
    smem = pl.BlockSpec(memory_space=pltpu.SMEM)
    limit = pltpu.CompilerParams(vmem_limit_bytes=32 * MIB)

    def route(flip):
        def target(c, here):
            return (here % 2) * Y + 2 * c + (here // 2 ^ flip)

        return [(c * Y + here, target(c, here)) for c in range(2) for here in range(Y)]

    payload = jax.ShapeDtypeStruct((2 * sources, local), jnp.bfloat16)
    loads = pl.pallas_call(
        pick_kernel,
        out_shape=(payload, payload),
        in_specs=[smem, anywhere],
        out_specs=(anywhere, anywhere),
        scratch_shapes=[pltpu.SemaphoreType.DMA((2,))],
        compiler_params=limit,
        name="pick",
    )(position, kernel.reshape(2, 2 * sources, local))
    blocks = [lax.ppermute(load, COLUMN, route(n)) for n, load in enumerate(loads)]
    def table(p, freqs):
        half = jax.ShapeDtypeStruct((kept, samples), jnp.bfloat16)
        return pl.pallas_call(
            functools.partial(table_kernel, p), out_shape=(half, half), compiler_params=limit, name=f"table{p}"
        )(freqs)

    freqs = freq_index.reshape(deep, X * Y)
    spec, rec_norm = pl.pallas_call(
        dft_kernel,
        out_shape=(
            jax.ShapeDtypeStruct((GROUP * X * deep, 128), jnp.bfloat16),
            jax.ShapeDtypeStruct((1, 1), jnp.float32),
        ),
        scratch_shapes=[
            pltpu.VMEM((2, kept, samples), jnp.float32),
            pltpu.VMEM((GROUP * X * deep, 128), jnp.float32),
        ],
        compiler_params=limit,
        name="dft",
    )(freqs, recorded.reshape(share * virtual, samples))

    spec = spec.reshape(deep, X * GROUP, 128)
    spec = lax.all_to_all(spec, "z", split_axis=0, concat_axis=0, tiled=True)
    spec, *blocks = lax.optimization_barrier((spec, *blocks))
    blocks = blocks + [lax.ppermute(b, "core", [(0, 1), (1, 0)]) for b in blocks]
    spec = lax.all_to_all(spec.transpose(1, 0, 2), SLAB, split_axis=0, concat_axis=0, tiled=True)

    spec = pl.pallas_call(
        gather_kernel,
        out_shape=jax.ShapeDtypeStruct((HV, 2 * sources), jnp.float32),
        scratch_shapes=[pltpu.VMEM((8 * X * deep, 128), jnp.float32)],
        compiler_params=limit,
        cost_estimate=pl.CostEstimate(flops=10**11, bytes_accessed=10**6, transcendentals=0),
        name="gather",
    )(spec)

    lines = 3 * deep + EXTRA
    vectors = pl.pallas_call(
        krylov_kernel,
        out_shape=jax.ShapeDtypeStruct((X * GROUP, lines, 128), jnp.bfloat16),
        in_specs=[smem] + [vmem] * 6,
        out_specs=vmem,
        scratch_shapes=[pltpu.VMEM((4 * local, 128), jnp.float32)],
        compiler_params=limit,
        name="krylov",
    )(position, rec_norm, spec, *blocks)
    vectors, freqs = lax.optimization_barrier((vectors, freqs))
    (hi0, lo0), (hi1, lo1) = table(0, freqs), table(1, freqs)
    back = lax.all_to_all(vectors, SLAB, split_axis=0, concat_axis=0, tiled=True)
    data = back[:, : 3 * deep].reshape(X * GROUP, 3, deep, 128).transpose(2, 0, 1, 3)
    data = data.reshape(deep, 3 * X * GROUP, 128)
    scal = back[:, 3 * deep].astype(jnp.float32).reshape(X, GROUP, 128)
    scal = jnp.sum(scal, axis=1).astype(jnp.bfloat16)
    scal = jnp.concatenate([scal, jnp.zeros_like(scal)], axis=0)
    send = jnp.concatenate([data, jnp.broadcast_to(scal, (deep, 2 * X, 128))], axis=1)
    got = lax.all_to_all(send, "z", split_axis=0, concat_axis=0, tiled=True).transpose(1, 0, 2)

    return pl.pallas_call(
        traces_kernel,
        out_shape=tuple(jax.ShapeDtypeStruct((share, virtual, samples), jnp.float32) for _ in range(2)),
        compiler_params=limit,
        name="traces",
    )(got, hi0, lo0, hi1, lo1)


def solution(mesh):
    devices = mesh.devices
    deep = devices.shape[0] // (2 * X)
    fine = Mesh(devices.reshape(deep, X, 2, devices.shape[1]), ("z", "x", "core", "rcv"))
    traces = P(("rcv", "z", "x", "core"), None, None)
    in_specs = (traces, P(("z", "x", "core"), None, None, "rcv"), P())
    return jax.shard_map(body, mesh=fine, in_specs=in_specs, out_specs=(traces, traces), check_vma=False)
```

```python
import functools
import math

import jax
import jax.numpy as jnp
from jax import lax
from jax.experimental import pallas as pl
from jax.experimental.pallas import tpu as pltpu
from jax.sharding import Mesh, PartitionSpec as P

X = 4
Y = 4
GROUP = 8
HV = 32
EXTRA = 16
HIGH = lax.Precision.HIGHEST
MIB = 1024 * 1024
COLUMN = ("core", "rcv")
SLAB = ("x", "core", "rcv")


def pick_kernel(idx_ref, k_ref, first_ref, second_ref, sems):
    upper = idx_ref[0] // 2
    copies = [
        pltpu.make_async_copy(k_ref.at[upper], first_ref, sems.at[0]),
        pltpu.make_async_copy(k_ref.at[1 - upper], second_ref, sems.at[1]),
    ]
    for copy in copies:
        copy.start()
    for copy in copies:
        copy.wait()


def angles(fr_ref, samples):
    unit = 2.0 * math.pi / samples
    fr = jnp.concatenate([fr_ref[:, n : n + 1] for n in range(fr_ref.shape[1])], axis=0)
    lane = lax.broadcasted_iota(jnp.int32, (fr.shape[0], 128), 1)
    fine = (fr * lane & (samples - 1)).astype(jnp.float32) * unit
    coarse = (fr * (lane * 128) & (samples - 1)).astype(jnp.float32) * unit
    factor = 1.0 / math.sqrt(samples)
    return jnp.cos(fine), jnp.sin(fine), jnp.cos(coarse) * factor, jnp.sin(coarse) * factor


def table_kernel(p, fr_ref, hi_ref, lo_ref):
    samples = hi_ref.shape[1]
    cos_f, sin_f, cos_c, sin_c = angles(fr_ref, samples)
    for a in range(samples // 128):
        ca, sa = cos_c[:, a : a + 1], sin_c[:, a : a + 1]
        part = slice(a * 128, (a + 1) * 128)
        value = ca * cos_f - sa * sin_f if p == 0 else -(sa * cos_f + ca * sin_f)
        top = value.astype(jnp.bfloat16)
        hi_ref[:, part] = top
        lo_ref[:, part] = (value - top.astype(jnp.float32)).astype(jnp.bfloat16)


def dft_kernel(fr_ref, rec_ref, out_ref, norm_ref, table, rows):
    deep = fr_ref.shape[0]
    samples = rec_ref.shape[1]
    cos_f, sin_f, cos_c, sin_c = angles(fr_ref, samples)
    for a in range(samples // 128):
        ca, sa = cos_c[:, a : a + 1], sin_c[:, a : a + 1]
        part = slice(a * 128, (a + 1) * 128)
        table[0, :, part] = ca * cos_f - sa * sin_f
        table[1, :, part] = -(sa * cos_f + ca * sin_f)
    rec = rec_ref[...]
    norm_ref[...] = jnp.sum(rec * rec, axis=(0, 1), keepdims=True)
    spec = [
        lax.dot_general(table[p], rec, (((1,), (1,)), ((), ())), precision=HIGH, preferred_element_type=jnp.float32)
        for p in range(2)
    ]
    for c in range(2):
        parts = [spec[p][:, (2 * src + c) * HV : (2 * src + c + 1) * HV] for src in range(2) for p in range(2)]
        both = jnp.concatenate(parts, axis=1)
        for x in range(X):
            for phi in range(Y):
                n = x * Y + phi
                start = x * GROUP + c * Y + phi
                rows[pl.ds(start, deep, stride=X * GROUP), :] = both[n * deep : (n + 1) * deep]
    out_ref[...] = rows[...].astype(jnp.bfloat16)


def quarter_turn(x):
    width = x.shape[1]
    even = lax.broadcasted_iota(jnp.int32, x.shape, 1) % 2 == 0
    return jnp.where(even, pltpu.roll(x, width - 1, 1), -pltpu.roll(x, 1, 1))


def total(x):
    return jnp.sum(x, axis=(0, 1), keepdims=True)


def length_of(x):
    return jnp.sqrt(total(x * x))


def inverse_of(x):
    return jnp.where(x > 1e-30, 1.0 / jnp.maximum(x, 1e-30), 0.0)


def both_turns(p):
    return jnp.concatenate([p, quarter_turn(p)], axis=0).astype(jnp.bfloat16)


def gather_kernel(u_ref, first_ref, second_ref, out_ref, part_ref, u_rows):
    deep = u_ref.shape[1]
    share = first_ref.shape[1]
    for x in range(X):
        for c in range(2):
            fields = [u_ref[x * GROUP + c * Y + ys].astype(jnp.float32) for ys in range(Y)]
            for g in range(4):
                both = jnp.concatenate([block[:, g * HV : (g + 1) * HV] for block in fields], axis=1)
                u_rows[pl.ds(x * 8 + c * 4 + g, deep, stride=8 * X), :] = both
    turned = u_rows[...].T
    u = jnp.concatenate([turned[ys * HV : (ys + 1) * HV] for ys in range(Y)], axis=1)
    out_ref[...] = u
    both = both_turns(u)
    part_ref[:, :share] = jnp.dot(both, first_ref[...], preferred_element_type=jnp.float32)
    part_ref[:, share:] = jnp.dot(both, second_ref[...], preferred_element_type=jnp.float32)


def krylov_kernel(idx_ref, norm_ref, u_ref, part_ref, *refs):
    k_refs, g_ref, q_rows = refs[:4], refs[4], refs[5]
    share = k_refs[0].shape[1]
    columns = share // 4
    y, core = idx_ref[0], idx_ref[1]
    near = lax.rem(y, 2) * 2
    quarters = [(near if j % 2 == 0 else 2 - near) + (core if j < 2 else 1 - core) for j in range(4)]

    def products(both, some):
        return [jnp.dot(both, k_ref[...], preferred_element_type=jnp.float32) for k_ref in some]

    def adjoint(p):
        return 0.5 * jnp.concatenate(products(both_turns(p), k_refs), axis=1)

    def forward(q):
        q = q.astype(jnp.bfloat16)
        w = sum(
            lax.dot_general(
                q[:, j * share : (j + 1) * share],
                k_refs[j][...],
                (((1,), (1,)), ((), ())),
                preferred_element_type=jnp.float32,
            )
            for j in range(4)
        )
        return 0.5 * (w[:HV] - quarter_turn(w[HV:]))

    def write(first, second, start, count):
        q_rows[...] = jnp.concatenate([first, second], axis=0).T
        for c in range(2):
            for j in range(4):
                base = j * share + 2 * c
                even = q_rows[pl.ds(base, columns, stride=4), :]
                odd = q_rows[pl.ds(base + 1, columns, stride=4), :]
                for n in range(count):
                    lanes = slice(n * 64, (n + 1) * 64)
                    both = jnp.concatenate([even[:, lanes], odd[:, lanes]], axis=1)
                    row = (start + n) * columns
                    g_ref[c * Y + quarters[j], row : row + columns, :] = both.astype(jnp.bfloat16)

    u = u_ref[...]
    length = length_of(u)
    scale = inverse_of(length)
    g1 = jnp.concatenate([part_ref[...]] + products(both_turns(u), k_refs[2:]), axis=1) * (0.5 * scale)
    a1 = length_of(g1)
    q1 = g1 * inverse_of(a1)
    h2 = forward(q1) - (a1 * scale) * u
    b2 = length_of(h2)
    p2 = h2 * inverse_of(b2)
    g2 = adjoint(p2) - b2 * q1
    a2 = length_of(g2)
    q2 = g2 * inverse_of(a2)
    write(q1, q2, 0, 2)
    h3 = forward(q2) - a2 * p2
    b3 = length_of(h3)
    p3 = h3 * inverse_of(b3)
    g3 = adjoint(p3) - b3 * q2
    a3 = length_of(g3)
    q3 = g3 * inverse_of(a3)
    write(q3, q3, 2, 1)

    lane = lax.broadcasted_iota(jnp.int32, (EXTRA, 128), 1)
    slot = lax.rem(lane, 64) // GROUP
    values = jnp.zeros((EXTRA, 128), jnp.float32)
    for n, value in enumerate((math.sqrt(2.0) * length, a1, b2, a2, b3, a3, norm_ref[...])):
        values = jnp.where(slot == n, value, values)
    hi = values.astype(jnp.bfloat16).astype(jnp.float32)
    scalars = jnp.where(lane < 64, hi, values - hi)
    scalars = jnp.where(lax.rem(lane, GROUP) == core * Y + y, scalars, 0.0).astype(jnp.bfloat16)
    for e in range(GROUP):
        g_ref[e, 3 * columns : 3 * columns + EXTRA, :] = scalars


def reduced_lsqr(s, a1, b2, a2, b3, a3, rec):
    def norm(*parts):
        return jnp.sqrt(total(sum(part * part for part in parts)))

    beta = jnp.sqrt(total(rec))
    y11 = s / beta
    w1 = jnp.sqrt(jnp.maximum(1.0 - total(y11 * y11), 0.0))
    x = a1 * y11
    alpha = norm(x)
    x11 = x / alpha
    res, diag = beta, alpha
    y21, y22, w2 = a1 * x11 - alpha * y11, b2 * x11, -alpha * w1
    beta = jnp.sqrt(total(y21 * y21 + y22 * y22) + w2 * w2)
    y21, y22, w2 = y21 / beta, y22 / beta, w2 / beta
    x21, x22 = a1 * y21 + b2 * y22 - beta * x11, a2 * y22
    alpha = norm(x21, x22)
    x21, x22 = x21 / alpha, x22 / alpha

    def rotate(res, diag, beta, alpha):
        rho = jnp.sqrt(diag * diag + beta * beta)
        c, sn = diag / rho, beta / rho
        return c * res / rho, sn * alpha / rho, sn * res, -c * alpha

    step, couple, res, diag = rotate(res, diag, beta, alpha)
    sol1 = step * x11
    dir1, dir2 = x21 - couple * x11, x22
    y31, y32, y33 = a1 * x21 - alpha * y21, b2 * x21 + a2 * x22 - alpha * y22, b3 * x22
    w3 = -alpha * w2
    beta = jnp.sqrt(total(y31 * y31 + y32 * y32 + y33 * y33) + w3 * w3)
    y31, y32, y33 = y31 / beta, y32 / beta, y33 / beta
    x31 = a1 * y31 + b2 * y32 - beta * x21
    x32 = a2 * y32 + b3 * y33 - beta * x22
    x33 = a3 * y33
    alpha = norm(x31, x32, x33)
    step, couple, res, diag = rotate(res, diag, beta, alpha)
    last = res * diag / alpha
    return (sol1 + step * dir1, step * dir2), (last * x31, last * x32, last * x33)


def traces_kernel(m_ref, hi0_ref, lo0_ref, hi1_ref, lo1_ref, sol_ref, res_ref):
    scal = m_ref[3 * GROUP].astype(jnp.float32)
    parts = [
        scal[:, n * GROUP : (n + 1) * GROUP] + scal[:, 64 + n * GROUP : 64 + (n + 1) * GROUP] for n in range(7)
    ]
    sol_c, res_c = reduced_lsqr(*parts)
    root = math.sqrt(2.0)
    sol_c, res_c = [root * w for w in sol_c], [root * w for w in res_c]
    lines = []
    for weights in (sol_c, res_c):
        for c in range(2):
            blocks = []
            for phi in range(Y):
                e = c * Y + phi
                blocks.append(
                    sum(w[:, e : e + 1] * m_ref[3 * e + n].astype(jnp.float32) for n, w in enumerate(weights))
                )
            turned = jnp.concatenate(blocks, axis=0).T
            for rr in range(2):
                lines.append(
                    jnp.concatenate([turned[(2 * rr + q) * HV : (2 * rr + q + 1) * HV] for q in range(2)], axis=1)
                )
    rows = jnp.concatenate(lines, axis=0)
    hi = rows.astype(jnp.bfloat16)
    lo = (rows - hi.astype(jnp.float32)).astype(jnp.bfloat16)
    thi = jnp.concatenate([hi0_ref[...], hi1_ref[...]], axis=0)
    tlo = jnp.concatenate([lo0_ref[...], lo1_ref[...]], axis=0)

    def dot(a, b):
        return jnp.dot(a, b, preferred_element_type=jnp.float32)

    out = dot(hi, thi) + (dot(hi, tlo) + dot(lo, thi))
    for n, ref in enumerate((sol_ref, res_ref)):
        for c in range(2):
            for rr in range(2):
                row = ((n * 2 + c) * 2 + rr) * HV
                ref[rr, c * HV : (c + 1) * HV, :] = out[row : row + HV]


def body(recorded, kernel, freq_index):
    share, virtual, samples = recorded.shape
    kept = freq_index.shape[0]
    deep = kept // (X * Y)
    sources, local = kernel.shape[1], kernel.shape[3]
    core = lax.axis_index("core")
    y = lax.axis_index("rcv")
    position = jnp.stack([y, core]).astype(jnp.int32)
    anywhere = pl.BlockSpec(memory_space=pl.ANY)
    vmem = pl.BlockSpec(memory_space=pltpu.VMEM)
    smem = pl.BlockSpec(memory_space=pltpu.SMEM)
    limit = pltpu.CompilerParams(vmem_limit_bytes=32 * MIB)

    def route(flip):
        def target(c, here):
            return (here % 2) * Y + 2 * c + (here // 2 ^ flip)

        return [(c * Y + here, target(c, here)) for c in range(2) for here in range(Y)]

    payload = jax.ShapeDtypeStruct((2 * sources, local), jnp.bfloat16)
    loads = pl.pallas_call(
        pick_kernel,
        out_shape=(payload, payload),
        in_specs=[smem, anywhere],
        out_specs=(anywhere, anywhere),
        scratch_shapes=[pltpu.SemaphoreType.DMA((2,))],
        compiler_params=limit,
        name="pick",
    )(position, kernel.reshape(2, 2 * sources, local))
    blocks = [lax.ppermute(load, COLUMN, route(n)) for n, load in enumerate(loads)]
    def table(p, freqs):
        half = jax.ShapeDtypeStruct((kept, samples), jnp.bfloat16)
        return pl.pallas_call(
            functools.partial(table_kernel, p), out_shape=(half, half), compiler_params=limit, name=f"table{p}"
        )(freqs)

    freqs = freq_index.reshape(deep, X * Y)
    spec, rec_norm = pl.pallas_call(
        dft_kernel,
        out_shape=(
            jax.ShapeDtypeStruct((GROUP * X * deep, 128), jnp.bfloat16),
            jax.ShapeDtypeStruct((1, 1), jnp.float32),
        ),
        scratch_shapes=[
            pltpu.VMEM((2, kept, samples), jnp.float32),
            pltpu.VMEM((GROUP * X * deep, 128), jnp.float32),
        ],
        compiler_params=limit,
        name="dft",
    )(freqs, recorded.reshape(share * virtual, samples))

    spec = spec.reshape(deep, X * GROUP, 128)
    spec = lax.all_to_all(spec, "z", split_axis=0, concat_axis=0, tiled=True)
    spec, *blocks = lax.optimization_barrier((spec, *blocks))
    blocks = blocks + [lax.ppermute(b, "core", [(0, 1), (1, 0)]) for b in blocks]
    spec = lax.all_to_all(spec.transpose(1, 0, 2), SLAB, split_axis=0, concat_axis=0, tiled=True)

    field, part = pl.pallas_call(
        gather_kernel,
        out_shape=(
            jax.ShapeDtypeStruct((HV, 2 * sources), jnp.float32),
            jax.ShapeDtypeStruct((2 * HV, 2 * local), jnp.float32),
        ),
        scratch_shapes=[pltpu.VMEM((8 * X * deep, 128), jnp.float32)],
        compiler_params=limit,
        cost_estimate=pl.CostEstimate(flops=10**11, bytes_accessed=10**6, transcendentals=0),
        name="gather",
    )(spec, *blocks[:2])

    columns = X * deep
    lines = 3 * columns + EXTRA
    vectors = pl.pallas_call(
        krylov_kernel,
        out_shape=jax.ShapeDtypeStruct((GROUP, lines, 128), jnp.bfloat16),
        in_specs=[smem] + [vmem] * 7,
        out_specs=vmem,
        scratch_shapes=[pltpu.VMEM((4 * local, 128), jnp.float32)],
        compiler_params=limit,
        name="krylov",
    )(position, rec_norm, field, part, *blocks)
    vectors, freqs = lax.optimization_barrier((vectors, freq_index.reshape(columns, Y)))
    (hi0, lo0), (hi1, lo1) = table(0, freqs), table(1, freqs)
    back = lax.all_to_all(vectors, COLUMN, split_axis=0, concat_axis=0, tiled=True)
    data = back[:, : 3 * columns].reshape(GROUP, 3, columns, 128).transpose(2, 0, 1, 3).reshape(columns, 24, 128)
    scal = jnp.sum(back[:, 3 * columns].astype(jnp.float32), axis=0).astype(jnp.bfloat16)
    scal = jnp.broadcast_to(scal, (columns, 2, 128))
    send = jnp.concatenate([data, scal], axis=1).reshape(columns, 13, 2, 128)
    got = lax.all_to_all(send, ("z", "x"), split_axis=0, concat_axis=0, tiled=True)
    got = got.reshape(columns, 26, 128).transpose(1, 0, 2)

    return pl.pallas_call(
        traces_kernel,
        out_shape=tuple(jax.ShapeDtypeStruct((share, virtual, samples), jnp.float32) for _ in range(2)),
        compiler_params=limit,
        name="traces",
    )(got, hi0, lo0, hi1, lo1)


def solution(mesh):
    devices = mesh.devices
    deep = devices.shape[0] // (2 * X)
    fine = Mesh(devices.reshape(deep, X, 2, devices.shape[1]), ("z", "x", "core", "rcv"))
    traces = P(("rcv", "z", "x", "core"), None, None)
    in_specs = (traces, P(("z", "x", "core"), None, None, "rcv"), P())
    return jax.shard_map(body, mesh=fine, in_specs=in_specs, out_specs=(traces, traces), check_vma=False)
```

```python
import functools
import math

import jax
import jax.numpy as jnp
from jax import lax
from jax.experimental import pallas as pl
from jax.experimental.pallas import tpu as pltpu
from jax.sharding import Mesh, PartitionSpec as P

X = 4
Y = 4
GROUP = 8
HV = 32
EXTRA = 8
HIGH = lax.Precision.HIGHEST
MIB = 1024 * 1024
COLUMN = ("core", "rcv")
SLAB = ("x", "core", "rcv")


def pick_kernel(idx_ref, k_ref, first_ref, second_ref, sems):
    upper = idx_ref[0] // 2
    copies = [
        pltpu.make_async_copy(k_ref.at[upper], first_ref, sems.at[0]),
        pltpu.make_async_copy(k_ref.at[1 - upper], second_ref, sems.at[1]),
    ]
    for copy in copies:
        copy.start()
    for copy in copies:
        copy.wait()


def angles(fr_ref, samples):
    unit = 2.0 * math.pi / samples
    chunks = samples // 128
    deep, groups = fr_ref.shape
    fr = jnp.concatenate([fr_ref[:, n : n + 1] for n in range(groups)], axis=0)
    lane = lax.broadcasted_iota(jnp.int32, (deep * groups, 128), 1)
    fine = (fr * lane & (samples - 1)).astype(jnp.float32) * unit
    wide = [jnp.broadcast_to(fr_ref[:, n : n + 1], (deep, chunks)) for n in range(groups)]
    wide = jnp.concatenate(wide, axis=1)
    step = lax.rem(lax.broadcasted_iota(jnp.int32, wide.shape, 1), chunks) * 128
    coarse = (wide * step & (samples - 1)).astype(jnp.float32) * unit
    factor = 1.0 / math.sqrt(samples)
    cos_c, sin_c = jnp.cos(coarse) * factor, jnp.sin(coarse) * factor

    def column(values, a):
        return jnp.concatenate([values[:, n * chunks + a : n * chunks + a + 1] for n in range(groups)], axis=0)

    pairs = [(column(cos_c, a), column(sin_c, a)) for a in range(chunks)]
    return jnp.cos(fine), jnp.sin(fine), pairs


def table_kernel(p, fr_ref, hi_ref, lo_ref):
    samples = hi_ref.shape[1]
    cos_f, sin_f, pairs = angles(fr_ref, samples)
    for a, (ca, sa) in enumerate(pairs):
        part = slice(a * 128, (a + 1) * 128)
        value = ca * cos_f - sa * sin_f if p == 0 else -(sa * cos_f + ca * sin_f)
        top = value.astype(jnp.bfloat16)
        hi_ref[:, part] = top
        lo_ref[:, part] = (value - top.astype(jnp.float32)).astype(jnp.bfloat16)


def dft_kernel(fr_ref, rec_ref, out_ref, norm_ref, table, rows):
    deep = fr_ref.shape[0]
    samples = rec_ref.shape[1]
    cos_f, sin_f, pairs = angles(fr_ref, samples)
    for a, (ca, sa) in enumerate(pairs):
        part = slice(a * 128, (a + 1) * 128)
        table[0, :, part] = ca * cos_f - sa * sin_f
        table[1, :, part] = -(sa * cos_f + ca * sin_f)
    rec = rec_ref[...]
    norm_ref[...] = jnp.sum(rec * rec, axis=(0, 1), keepdims=True)
    spec = [
        lax.dot_general(table[p], rec, (((1,), (1,)), ((), ())), precision=HIGH, preferred_element_type=jnp.float32)
        for p in range(2)
    ]
    for c in range(2):
        parts = [spec[p][:, (2 * src + c) * HV : (2 * src + c + 1) * HV] for src in range(2) for p in range(2)]
        both = jnp.concatenate(parts, axis=1)
        for x in range(X):
            for phi in range(Y):
                n = x * Y + phi
                start = x * GROUP + c * Y + phi
                rows[pl.ds(start, deep, stride=X * GROUP), :] = both[n * deep : (n + 1) * deep]
    out_ref[...] = rows[...].astype(jnp.bfloat16)


def quarter_turn(x):
    width = x.shape[1]
    even = lax.broadcasted_iota(jnp.int32, x.shape, 1) % 2 == 0
    return jnp.where(even, pltpu.roll(x, width - 1, 1), -pltpu.roll(x, 1, 1))


def total(x):
    return jnp.sum(x, axis=(0, 1), keepdims=True)


def length_of(x):
    return jnp.sqrt(total(x * x))


def inverse_of(x):
    return jnp.where(x > 1e-30, 1.0 / jnp.maximum(x, 1e-30), 0.0)


def gather_kernel(u_ref, out_ref, u_rows):
    deep = u_ref.shape[1]
    for x in range(X):
        for c in range(2):
            fields = [u_ref[x * GROUP + c * Y + ys].astype(jnp.float32) for ys in range(Y)]
            for g in range(4):
                both = jnp.concatenate([block[:, g * HV : (g + 1) * HV] for block in fields], axis=1)
                u_rows[pl.ds(x * 8 + c * 4 + g, deep, stride=8 * X), :] = both
    turned = u_rows[...].T
    out_ref[...] = jnp.concatenate([turned[ys * HV : (ys + 1) * HV] for ys in range(Y)], axis=1)


def krylov_kernel(idx_ref, norm_ref, u_ref, *refs):
    k_refs, g_ref = refs[:4], refs[4]
    (q_rows,) = refs[5:]
    deep = (g_ref.shape[1] - EXTRA) // 3
    share = k_refs[0].shape[1]
    y, core = idx_ref[0], idx_ref[1]
    near = lax.rem(y, 2) * 2
    quarters = [(near if j % 2 == 0 else 2 - near) + (core if j < 2 else 1 - core) for j in range(4)]

    u = u_ref[...]

    def adjoint(p):
        both = jnp.concatenate([p, quarter_turn(p)], axis=0).astype(jnp.bfloat16)
        parts = [jnp.dot(both, k_ref[...], preferred_element_type=jnp.float32) for k_ref in k_refs]
        return 0.5 * jnp.concatenate(parts, axis=1)

    def forward(q):
        q = q.astype(jnp.bfloat16)
        w = sum(
            lax.dot_general(
                q[:, j * share : (j + 1) * share],
                k_refs[j][...],
                (((1,), (1,)), ((), ())),
                preferred_element_type=jnp.float32,
            )
            for j in range(4)
        )
        return 0.5 * (w[:HV] - quarter_turn(w[HV:]))

    length = length_of(u)
    scale = inverse_of(length)
    g1 = adjoint(u) * scale
    a1 = length_of(g1)
    q1 = g1 * inverse_of(a1)
    h2 = forward(q1) - (a1 * scale) * u
    b2 = length_of(h2)
    p2 = h2 * inverse_of(b2)
    g2 = adjoint(p2) - b2 * q1
    a2 = length_of(g2)
    q2 = g2 * inverse_of(a2)
    h3 = forward(q2) - a2 * p2
    b3 = length_of(h3)
    p3 = h3 * inverse_of(b3)
    g3 = adjoint(p3) - b3 * q2
    a3 = length_of(g3)
    q3 = g3 * inverse_of(a3)

    lane = lax.broadcasted_iota(jnp.int32, (EXTRA, 128), 1)
    slot = lax.rem(lane, 64) // GROUP
    values = jnp.zeros((EXTRA, 128), jnp.float32)
    for n, value in enumerate((math.sqrt(2.0) * length, a1, b2, a2, b3, a3, norm_ref[...])):
        values = jnp.where(slot == n, value, values)
    hi = values.astype(jnp.bfloat16).astype(jnp.float32)
    scalars = jnp.where(lane < 64, hi, values - hi)
    scalars = jnp.where(lax.rem(lane, GROUP) == core * Y + y, scalars, 0.0).astype(jnp.bfloat16)

    for pair in range(2):
        first, second = ((q1, q2), (q3, q3))[pair]
        q_rows[...] = jnp.concatenate([first, second], axis=0).T
        for x in range(X):
            for c in range(2):
                for j in range(4):
                    base = j * share + x * 4 + c * 2
                    even = q_rows[pl.ds(base, deep, stride=4 * X), :]
                    odd = q_rows[pl.ds(base + 1, deep, stride=4 * X), :]
                    for inner in range(2 - pair):
                        lanes = slice(inner * 64, (inner + 1) * 64)
                        both = jnp.concatenate([even[:, lanes], odd[:, lanes]], axis=1)
                        row = (2 * pair + inner) * deep
                        g_ref[x * GROUP + c * Y + quarters[j], row : row + deep, :] = both.astype(jnp.bfloat16)
    for e in range(X * GROUP):
        g_ref[e, 3 * deep : 3 * deep + EXTRA, :] = scalars


def reduced_lsqr(s, a1, b2, a2, b3, a3, rec):
    def norm(*parts):
        return jnp.sqrt(total(sum(part * part for part in parts)))

    beta = jnp.sqrt(total(rec))
    y11 = s / beta
    w1 = jnp.sqrt(jnp.maximum(1.0 - total(y11 * y11), 0.0))
    x = a1 * y11
    alpha = norm(x)
    x11 = x / alpha
    res, diag = beta, alpha
    y21, y22, w2 = a1 * x11 - alpha * y11, b2 * x11, -alpha * w1
    beta = jnp.sqrt(total(y21 * y21 + y22 * y22) + w2 * w2)
    y21, y22, w2 = y21 / beta, y22 / beta, w2 / beta
    x21, x22 = a1 * y21 + b2 * y22 - beta * x11, a2 * y22
    alpha = norm(x21, x22)
    x21, x22 = x21 / alpha, x22 / alpha

    def rotate(res, diag, beta, alpha):
        rho = jnp.sqrt(diag * diag + beta * beta)
        c, sn = diag / rho, beta / rho
        return c * res / rho, sn * alpha / rho, sn * res, -c * alpha

    step, couple, res, diag = rotate(res, diag, beta, alpha)
    sol1 = step * x11
    dir1, dir2 = x21 - couple * x11, x22
    y31, y32, y33 = a1 * x21 - alpha * y21, b2 * x21 + a2 * x22 - alpha * y22, b3 * x22
    w3 = -alpha * w2
    beta = jnp.sqrt(total(y31 * y31 + y32 * y32 + y33 * y33) + w3 * w3)
    y31, y32, y33 = y31 / beta, y32 / beta, y33 / beta
    x31 = a1 * y31 + b2 * y32 - beta * x21
    x32 = a2 * y32 + b3 * y33 - beta * x22
    x33 = a3 * y33
    alpha = norm(x31, x32, x33)
    step, couple, res, diag = rotate(res, diag, beta, alpha)
    last = res * diag / alpha
    return (sol1 + step * dir1, step * dir2), (last * x31, last * x32, last * x33)


def traces_kernel(m_ref, hi0_ref, lo0_ref, hi1_ref, lo1_ref, sol_ref, res_ref):
    scal = [m_ref[3 * X * GROUP + x].astype(jnp.float32) for x in range(X)]
    parts = []
    for n in range(7):
        top, low = n * GROUP, 64 + n * GROUP
        parts.append(
            jnp.concatenate([sc[:, top : top + GROUP] + sc[:, low : low + GROUP] for sc in scal], axis=1)
        )
    sol_c, res_c = reduced_lsqr(*parts)
    root = math.sqrt(2.0)
    sol_c, res_c = [root * w for w in sol_c], [root * w for w in res_c]
    lines = []
    for weights in (sol_c, res_c):
        for c in range(2):
            blocks = []
            for x in range(X):
                for phi in range(Y):
                    e = x * GROUP + c * Y + phi
                    blocks.append(
                        sum(w[:, e : e + 1] * m_ref[3 * e + n].astype(jnp.float32) for n, w in enumerate(weights))
                    )
            turned = jnp.concatenate(blocks, axis=0).T
            for rr in range(2):
                lines.append(
                    jnp.concatenate([turned[(2 * rr + q) * HV : (2 * rr + q + 1) * HV] for q in range(2)], axis=1)
                )
    rows = jnp.concatenate(lines, axis=0)
    hi = rows.astype(jnp.bfloat16)
    lo = (rows - hi.astype(jnp.float32)).astype(jnp.bfloat16)
    thi = jnp.concatenate([hi0_ref[...], hi1_ref[...]], axis=0)
    tlo = jnp.concatenate([lo0_ref[...], lo1_ref[...]], axis=0)

    def dot(a, b):
        return jnp.dot(a, b, preferred_element_type=jnp.float32)

    out = dot(hi, thi) + (dot(hi, tlo) + dot(lo, thi))
    for n, ref in enumerate((sol_ref, res_ref)):
        for c in range(2):
            for rr in range(2):
                row = ((n * 2 + c) * 2 + rr) * HV
                ref[rr, c * HV : (c + 1) * HV, :] = out[row : row + HV]


def body(recorded, kernel, freq_index):
    share, virtual, samples = recorded.shape
    kept = freq_index.shape[0]
    deep = kept // (X * Y)
    sources, local = kernel.shape[1], kernel.shape[3]
    core = lax.axis_index("core")
    y = lax.axis_index("rcv")
    position = jnp.stack([y, core]).astype(jnp.int32)
    anywhere = pl.BlockSpec(memory_space=pl.ANY)
    vmem = pl.BlockSpec(memory_space=pltpu.VMEM)
    smem = pl.BlockSpec(memory_space=pltpu.SMEM)
    limit = pltpu.CompilerParams(vmem_limit_bytes=32 * MIB)

    def route(flip):
        def target(c, here):
            return (here % 2) * Y + 2 * c + (here // 2 ^ flip)

        return [(c * Y + here, target(c, here)) for c in range(2) for here in range(Y)]

    payload = jax.ShapeDtypeStruct((2 * sources, local), jnp.bfloat16)
    loads = pl.pallas_call(
        pick_kernel,
        out_shape=(payload, payload),
        in_specs=[smem, anywhere],
        out_specs=(anywhere, anywhere),
        scratch_shapes=[pltpu.SemaphoreType.DMA((2,))],
        compiler_params=limit,
        name="pick",
    )(position, kernel.reshape(2, 2 * sources, local))
    blocks = [lax.ppermute(load, COLUMN, route(n)) for n, load in enumerate(loads)]
    def table(p, freqs):
        half = jax.ShapeDtypeStruct((kept, samples), jnp.bfloat16)
        return pl.pallas_call(
            functools.partial(table_kernel, p), out_shape=(half, half), compiler_params=limit, name=f"table{p}"
        )(freqs)

    freqs = freq_index.reshape(deep, X * Y)
    spec, rec_norm = pl.pallas_call(
        dft_kernel,
        out_shape=(
            jax.ShapeDtypeStruct((GROUP * X * deep, 128), jnp.bfloat16),
            jax.ShapeDtypeStruct((1, 1), jnp.float32),
        ),
        scratch_shapes=[
            pltpu.VMEM((2, kept, samples), jnp.float32),
            pltpu.VMEM((GROUP * X * deep, 128), jnp.float32),
        ],
        compiler_params=limit,
        name="dft",
    )(freqs, recorded.reshape(share * virtual, samples))

    spec = spec.reshape(deep, X * GROUP, 128)
    spec = lax.all_to_all(spec, "z", split_axis=0, concat_axis=0, tiled=True)
    spec, *blocks = lax.optimization_barrier((spec, *blocks))
    blocks = blocks + [lax.ppermute(b, "core", [(0, 1), (1, 0)]) for b in blocks]
    spec = lax.all_to_all(spec.transpose(1, 0, 2), SLAB, split_axis=0, concat_axis=0, tiled=True)

    spec = pl.pallas_call(
        gather_kernel,
        out_shape=jax.ShapeDtypeStruct((HV, 2 * sources), jnp.float32),
        scratch_shapes=[pltpu.VMEM((8 * X * deep, 128), jnp.float32)],
        compiler_params=limit,
        cost_estimate=pl.CostEstimate(flops=10**11, bytes_accessed=10**6, transcendentals=0),
        name="gather",
    )(spec)

    lines = 3 * deep + EXTRA
    vectors = pl.pallas_call(
        krylov_kernel,
        out_shape=jax.ShapeDtypeStruct((X * GROUP, lines, 128), jnp.bfloat16),
        in_specs=[smem] + [vmem] * 6,
        out_specs=vmem,
        scratch_shapes=[pltpu.VMEM((4 * local, 128), jnp.float32)],
        compiler_params=limit,
        name="krylov",
    )(position, rec_norm, spec, *blocks)
    vectors, freqs = lax.optimization_barrier((vectors, freqs))
    (hi0, lo0), (hi1, lo1) = table(0, freqs), table(1, freqs)
    back = lax.all_to_all(vectors, SLAB, split_axis=0, concat_axis=0, tiled=True)
    data = back[:, : 3 * deep].reshape(X * GROUP, 3, deep, 128).transpose(2, 0, 1, 3)
    data = data.reshape(deep, 3 * X * GROUP, 128)
    scal = back[:, 3 * deep].astype(jnp.float32).reshape(X, GROUP, 128)
    scal = jnp.sum(scal, axis=1).astype(jnp.bfloat16)
    scal = jnp.concatenate([scal, jnp.zeros_like(scal)], axis=0)
    send = jnp.concatenate([data, jnp.broadcast_to(scal, (deep, 2 * X, 128))], axis=1)
    got = lax.all_to_all(send, "z", split_axis=0, concat_axis=0, tiled=True).transpose(1, 0, 2)

    return pl.pallas_call(
        traces_kernel,
        out_shape=tuple(jax.ShapeDtypeStruct((share, virtual, samples), jnp.float32) for _ in range(2)),
        compiler_params=limit,
        name="traces",
    )(got, hi0, lo0, hi1, lo1)


def solution(mesh):
    devices = mesh.devices
    deep = devices.shape[0] // (2 * X)
    fine = Mesh(devices.reshape(deep, X, 2, devices.shape[1]), ("z", "x", "core", "rcv"))
    traces = P(("rcv", "z", "x", "core"), None, None)
    in_specs = (traces, P(("z", "x", "core"), None, None, "rcv"), P())
    return jax.shard_map(body, mesh=fine, in_specs=in_specs, out_specs=(traces, traces), check_vma=False)
```

```python
import functools
import math

import jax
import jax.numpy as jnp
from jax import lax
from jax.experimental import pallas as pl
from jax.experimental.pallas import tpu as pltpu
from jax.sharding import Mesh, PartitionSpec as P

X = 4
Y = 4
GROUP = 8
HV = 32
EXTRA = 16
HIGH = lax.Precision.HIGHEST
MIB = 1024 * 1024
COLUMN = ("core", "rcv")
SLAB = ("x", "core", "rcv")


def pick_kernel(idx_ref, k_ref, first_ref, second_ref, sems):
    upper = idx_ref[0] // 2
    copies = [
        pltpu.make_async_copy(k_ref.at[upper], first_ref, sems.at[0]),
        pltpu.make_async_copy(k_ref.at[1 - upper], second_ref, sems.at[1]),
    ]
    for copy in copies:
        copy.start()
    for copy in copies:
        copy.wait()


def angles(fr_ref, samples):
    unit = 2.0 * math.pi / samples
    chunks = samples // 128
    deep, groups = fr_ref.shape
    fr = jnp.concatenate([fr_ref[:, n : n + 1] for n in range(groups)], axis=0)
    lane = lax.broadcasted_iota(jnp.int32, (deep * groups, 128), 1)
    fine = (fr * lane & (samples - 1)).astype(jnp.float32) * unit
    wide = [jnp.broadcast_to(fr_ref[:, n : n + 1], (deep, chunks)) for n in range(groups)]
    wide = jnp.concatenate(wide, axis=1)
    step = lax.rem(lax.broadcasted_iota(jnp.int32, wide.shape, 1), chunks) * 128
    coarse = (wide * step & (samples - 1)).astype(jnp.float32) * unit
    factor = 1.0 / math.sqrt(samples)
    cos_c, sin_c = jnp.cos(coarse) * factor, jnp.sin(coarse) * factor

    def column(values, a):
        return jnp.concatenate([values[:, n * chunks + a : n * chunks + a + 1] for n in range(groups)], axis=0)

    pairs = [(column(cos_c, a), column(sin_c, a)) for a in range(chunks)]
    return jnp.cos(fine), jnp.sin(fine), pairs


def table_kernel(p, fr_ref, hi_ref, lo_ref):
    samples = hi_ref.shape[1]
    cos_f, sin_f, pairs = angles(fr_ref, samples)
    for a, (ca, sa) in enumerate(pairs):
        part = slice(a * 128, (a + 1) * 128)
        value = ca * cos_f - sa * sin_f if p == 0 else -(sa * cos_f + ca * sin_f)
        top = value.astype(jnp.bfloat16)
        hi_ref[:, part] = top
        lo_ref[:, part] = (value - top.astype(jnp.float32)).astype(jnp.bfloat16)


def dft_kernel(fr_ref, rec_ref, out_ref, norm_ref, table, rows):
    deep = fr_ref.shape[0]
    samples = rec_ref.shape[1]
    cos_f, sin_f, pairs = angles(fr_ref, samples)
    for a, (ca, sa) in enumerate(pairs):
        part = slice(a * 128, (a + 1) * 128)
        table[0, :, part] = ca * cos_f - sa * sin_f
        table[1, :, part] = -(sa * cos_f + ca * sin_f)
    rec = rec_ref[...]
    norm_ref[...] = jnp.sum(rec * rec, axis=(0, 1), keepdims=True)
    spec = [
        lax.dot_general(table[p], rec, (((1,), (1,)), ((), ())), precision=HIGH, preferred_element_type=jnp.float32)
        for p in range(2)
    ]
    for c in range(2):
        parts = [spec[p][:, (2 * src + c) * HV : (2 * src + c + 1) * HV] for src in range(2) for p in range(2)]
        both = jnp.concatenate(parts, axis=1)
        for x in range(X):
            for phi in range(Y):
                n = x * Y + phi
                start = x * GROUP + c * Y + phi
                rows[pl.ds(start, deep, stride=X * GROUP), :] = both[n * deep : (n + 1) * deep]
    out_ref[...] = rows[...].astype(jnp.bfloat16)


def quarter_turn(x):
    width = x.shape[1]
    even = lax.broadcasted_iota(jnp.int32, x.shape, 1) % 2 == 0
    return jnp.where(even, pltpu.roll(x, width - 1, 1), -pltpu.roll(x, 1, 1))


def total(x):
    return jnp.sum(x, axis=(0, 1), keepdims=True)


def length_of(x):
    return jnp.sqrt(total(x * x))


def inverse_of(x):
    return jnp.where(x > 1e-30, 1.0 / jnp.maximum(x, 1e-30), 0.0)


def gather_kernel(u_ref, out_ref, u_rows):
    deep = u_ref.shape[1]
    for x in range(X):
        for c in range(2):
            fields = [u_ref[x * GROUP + c * Y + ys].astype(jnp.float32) for ys in range(Y)]
            for g in range(4):
                both = jnp.concatenate([block[:, g * HV : (g + 1) * HV] for block in fields], axis=1)
                u_rows[pl.ds(x * 8 + c * 4 + g, deep, stride=8 * X), :] = both
    turned = u_rows[...].T
    out_ref[...] = jnp.concatenate([turned[ys * HV : (ys + 1) * HV] for ys in range(Y)], axis=1)


def krylov_kernel(idx_ref, norm_ref, u_ref, *refs):
    k_refs, g_ref = refs[:4], refs[4]
    (q_rows,) = refs[5:]
    deep = (g_ref.shape[1] - EXTRA) // 3
    share = k_refs[0].shape[1]
    y, core = idx_ref[0], idx_ref[1]
    near = lax.rem(y, 2) * 2
    quarters = [(near if j % 2 == 0 else 2 - near) + (core if j < 2 else 1 - core) for j in range(4)]

    u = u_ref[...]

    def adjoint(p):
        both = jnp.concatenate([p, quarter_turn(p)], axis=0).astype(jnp.bfloat16)
        parts = [jnp.dot(both, k_ref[...], preferred_element_type=jnp.float32) for k_ref in k_refs]
        return 0.5 * jnp.concatenate(parts, axis=1)

    def forward(q):
        q = q.astype(jnp.bfloat16)
        w = sum(
            lax.dot_general(
                q[:, j * share : (j + 1) * share],
                k_refs[j][...],
                (((1,), (1,)), ((), ())),
                preferred_element_type=jnp.float32,
            )
            for j in range(4)
        )
        return 0.5 * (w[:HV] - quarter_turn(w[HV:]))

    length = length_of(u)
    scale = inverse_of(length)
    g1 = adjoint(u) * scale
    a1 = length_of(g1)
    q1 = g1 * inverse_of(a1)
    h2 = forward(q1) - (a1 * scale) * u
    b2 = length_of(h2)
    p2 = h2 * inverse_of(b2)
    g2 = adjoint(p2) - b2 * q1
    a2 = length_of(g2)
    q2 = g2 * inverse_of(a2)
    h3 = forward(q2) - a2 * p2
    b3 = length_of(h3)
    p3 = h3 * inverse_of(b3)
    g3 = adjoint(p3) - b3 * q2
    a3 = length_of(g3)
    q3 = g3 * inverse_of(a3)

    lane = lax.broadcasted_iota(jnp.int32, (EXTRA, 128), 1)
    slot = lax.rem(lane, 64) // GROUP
    values = jnp.zeros((EXTRA, 128), jnp.float32)
    for n, value in enumerate((math.sqrt(2.0) * length, a1, b2, a2, b3, a3, norm_ref[...])):
        values = jnp.where(slot == n, value, values)
    hi = values.astype(jnp.bfloat16).astype(jnp.float32)
    scalars = jnp.where(lane < 64, hi, values - hi)
    scalars = jnp.where(lax.rem(lane, GROUP) == core * Y + y, scalars, 0.0).astype(jnp.bfloat16)

    for pair in range(2):
        first, second = ((q1, q2), (q3, q3))[pair]
        q_rows[...] = jnp.concatenate([first, second], axis=0).T
        for x in range(X):
            for c in range(2):
                for j in range(4):
                    base = j * share + x * 4 + c * 2
                    even = q_rows[pl.ds(base, deep, stride=4 * X), :]
                    odd = q_rows[pl.ds(base + 1, deep, stride=4 * X), :]
                    for inner in range(2 - pair):
                        lanes = slice(inner * 64, (inner + 1) * 64)
                        both = jnp.concatenate([even[:, lanes], odd[:, lanes]], axis=1)
                        row = (2 * pair + inner) * deep
                        g_ref[x * GROUP + c * Y + quarters[j], row : row + deep, :] = both.astype(jnp.bfloat16)
    for e in range(X * GROUP):
        g_ref[e, 3 * deep : 3 * deep + EXTRA, :] = scalars


def reduced_lsqr(s, a1, b2, a2, b3, a3, rec):
    def norm(*parts):
        return jnp.sqrt(total(sum(part * part for part in parts)))

    beta = jnp.sqrt(total(rec))
    y11 = s / beta
    w1 = jnp.sqrt(jnp.maximum(1.0 - total(y11 * y11), 0.0))
    x = a1 * y11
    alpha = norm(x)
    x11 = x / alpha
    res, diag = beta, alpha
    y21, y22, w2 = a1 * x11 - alpha * y11, b2 * x11, -alpha * w1
    beta = jnp.sqrt(total(y21 * y21 + y22 * y22) + w2 * w2)
    y21, y22, w2 = y21 / beta, y22 / beta, w2 / beta
    x21, x22 = a1 * y21 + b2 * y22 - beta * x11, a2 * y22
    alpha = norm(x21, x22)
    x21, x22 = x21 / alpha, x22 / alpha

    def rotate(res, diag, beta, alpha):
        rho = jnp.sqrt(diag * diag + beta * beta)
        c, sn = diag / rho, beta / rho
        return c * res / rho, sn * alpha / rho, sn * res, -c * alpha

    step, couple, res, diag = rotate(res, diag, beta, alpha)
    sol1 = step * x11
    dir1, dir2 = x21 - couple * x11, x22
    y31, y32, y33 = a1 * x21 - alpha * y21, b2 * x21 + a2 * x22 - alpha * y22, b3 * x22
    w3 = -alpha * w2
    beta = jnp.sqrt(total(y31 * y31 + y32 * y32 + y33 * y33) + w3 * w3)
    y31, y32, y33 = y31 / beta, y32 / beta, y33 / beta
    x31 = a1 * y31 + b2 * y32 - beta * x21
    x32 = a2 * y32 + b3 * y33 - beta * x22
    x33 = a3 * y33
    alpha = norm(x31, x32, x33)
    step, couple, res, diag = rotate(res, diag, beta, alpha)
    last = res * diag / alpha
    return (sol1 + step * dir1, step * dir2), (last * x31, last * x32, last * x33)


def traces_kernel(m_ref, hi0_ref, lo0_ref, hi1_ref, lo1_ref, sol_ref, res_ref):
    scal = [m_ref[3 * X * GROUP + x].astype(jnp.float32) for x in range(X)]
    parts = []
    for n in range(7):
        top, low = n * GROUP, 64 + n * GROUP
        parts.append(
            jnp.concatenate([sc[:, top : top + GROUP] + sc[:, low : low + GROUP] for sc in scal], axis=1)
        )
    sol_c, res_c = reduced_lsqr(*parts)
    root = math.sqrt(2.0)
    sol_c, res_c = [root * w for w in sol_c], [root * w for w in res_c]
    lines = []
    for weights in (sol_c, res_c):
        for c in range(2):
            blocks = []
            for x in range(X):
                for phi in range(Y):
                    e = x * GROUP + c * Y + phi
                    blocks.append(
                        sum(w[:, e : e + 1] * m_ref[3 * e + n].astype(jnp.float32) for n, w in enumerate(weights))
                    )
            turned = jnp.concatenate(blocks, axis=0).T
            for rr in range(2):
                lines.append(
                    jnp.concatenate([turned[(2 * rr + q) * HV : (2 * rr + q + 1) * HV] for q in range(2)], axis=1)
                )
    rows = jnp.concatenate(lines, axis=0)
    hi = rows.astype(jnp.bfloat16)
    lo = (rows - hi.astype(jnp.float32)).astype(jnp.bfloat16)
    thi = jnp.concatenate([hi0_ref[...], hi1_ref[...]], axis=0)
    tlo = jnp.concatenate([lo0_ref[...], lo1_ref[...]], axis=0)

    def dot(a, b):
        return jnp.dot(a, b, preferred_element_type=jnp.float32)

    out = dot(hi, thi) + (dot(hi, tlo) + dot(lo, thi))
    for n, ref in enumerate((sol_ref, res_ref)):
        for c in range(2):
            for rr in range(2):
                row = ((n * 2 + c) * 2 + rr) * HV
                ref[rr, c * HV : (c + 1) * HV, :] = out[row : row + HV]


def body(recorded, kernel, freq_index):
    share, virtual, samples = recorded.shape
    kept = freq_index.shape[0]
    deep = kept // (X * Y)
    sources, local = kernel.shape[1], kernel.shape[3]
    core = lax.axis_index("core")
    y = lax.axis_index("rcv")
    position = jnp.stack([y, core]).astype(jnp.int32)
    anywhere = pl.BlockSpec(memory_space=pl.ANY)
    vmem = pl.BlockSpec(memory_space=pltpu.VMEM)
    smem = pl.BlockSpec(memory_space=pltpu.SMEM)
    limit = pltpu.CompilerParams(vmem_limit_bytes=32 * MIB)

    def route(flip):
        def target(c, here):
            return (here % 2) * Y + 2 * c + (here // 2 ^ flip)

        return [(c * Y + here, target(c, here)) for c in range(2) for here in range(Y)]

    payload = jax.ShapeDtypeStruct((2 * sources, local), jnp.bfloat16)
    loads = pl.pallas_call(
        pick_kernel,
        out_shape=(payload, payload),
        in_specs=[smem, anywhere],
        out_specs=(anywhere, anywhere),
        scratch_shapes=[pltpu.SemaphoreType.DMA((2,))],
        compiler_params=limit,
        name="pick",
    )(position, kernel.reshape(2, 2 * sources, local))
    blocks = [lax.ppermute(load, COLUMN, route(n)) for n, load in enumerate(loads)]
    def table(p, freqs):
        half = jax.ShapeDtypeStruct((kept, samples), jnp.bfloat16)
        return pl.pallas_call(
            functools.partial(table_kernel, p), out_shape=(half, half), compiler_params=limit, name=f"table{p}"
        )(freqs)

    freqs = freq_index.reshape(deep, X * Y)
    spec, rec_norm = pl.pallas_call(
        dft_kernel,
        out_shape=(
            jax.ShapeDtypeStruct((GROUP * X * deep, 128), jnp.bfloat16),
            jax.ShapeDtypeStruct((1, 1), jnp.float32),
        ),
        scratch_shapes=[
            pltpu.VMEM((2, kept, samples), jnp.float32),
            pltpu.VMEM((GROUP * X * deep, 128), jnp.float32),
        ],
        compiler_params=limit,
        name="dft",
    )(freqs, recorded.reshape(share * virtual, samples))

    spec = spec.reshape(deep, X * GROUP, 128)
    spec = lax.all_to_all(spec, "z", split_axis=0, concat_axis=0, tiled=True)
    spec, *blocks = lax.optimization_barrier((spec, *blocks))
    blocks = blocks + [lax.ppermute(b, "core", [(0, 1), (1, 0)]) for b in blocks]
    spec = lax.all_to_all(spec.transpose(1, 0, 2), SLAB, split_axis=0, concat_axis=0, tiled=True)

    spec = pl.pallas_call(
        gather_kernel,
        out_shape=jax.ShapeDtypeStruct((HV, 2 * sources), jnp.float32),
        scratch_shapes=[pltpu.VMEM((8 * X * deep, 128), jnp.float32)],
        compiler_params=limit,
        cost_estimate=pl.CostEstimate(flops=10**11, bytes_accessed=10**6, transcendentals=0),
        name="gather",
    )(spec)

    lines = 3 * deep + EXTRA
    vectors = pl.pallas_call(
        krylov_kernel,
        out_shape=jax.ShapeDtypeStruct((X * GROUP, lines, 128), jnp.bfloat16),
        in_specs=[smem] + [vmem] * 6,
        out_specs=vmem,
        scratch_shapes=[pltpu.VMEM((4 * local, 128), jnp.float32)],
        compiler_params=limit,
        name="krylov",
    )(position, rec_norm, spec, *blocks)
    vectors, freqs = lax.optimization_barrier((vectors, freqs))
    (hi0, lo0), (hi1, lo1) = table(0, freqs), table(1, freqs)
    back = lax.all_to_all(vectors, SLAB, split_axis=0, concat_axis=0, tiled=True)
    data = back[:, : 3 * deep].reshape(X * GROUP, 3, deep, 128).transpose(2, 0, 1, 3)
    data = data.reshape(deep, 3 * X * GROUP, 128)
    scal = back[:, 3 * deep].astype(jnp.float32).reshape(X, GROUP, 128)
    scal = jnp.sum(scal, axis=1).astype(jnp.bfloat16)
    scal = jnp.concatenate([scal, jnp.zeros_like(scal)], axis=0)
    send = jnp.concatenate([data, jnp.broadcast_to(scal, (deep, 2 * X, 128))], axis=1)
    got = lax.all_to_all(send, "z", split_axis=0, concat_axis=0, tiled=True).transpose(1, 0, 2)

    return pl.pallas_call(
        traces_kernel,
        out_shape=tuple(jax.ShapeDtypeStruct((share, virtual, samples), jnp.float32) for _ in range(2)),
        compiler_params=limit,
        name="traces",
    )(got, hi0, lo0, hi1, lo1)


def solution(mesh):
    devices = mesh.devices
    deep = devices.shape[0] // (2 * X)
    fine = Mesh(devices.reshape(deep, X, 2, devices.shape[1]), ("z", "x", "core", "rcv"))
    traces = P(("rcv", "z", "x", "core"), None, None)
    in_specs = (traces, P(("z", "x", "core"), None, None, "rcv"), P())
    return jax.shard_map(body, mesh=fine, in_specs=in_specs, out_specs=(traces, traces), check_vma=False)
```
